128 devices in a mesh: head: 8 (over x_lo, z), inner: 4 (over y), outer: 4 (over x_hi, core).
Axes of the slice: x: 4 (x_hi: 2, x_lo: 2; x = x_hi * 2 + x_lo), y: 4, z: 4, core: 2. Of those that a mesh axis runs over, the one named last changes fastest.
Arguments:
- queries: bfloat16 [16, 1024, 2048], P(('inner', 'outer'), 'head'), may hold values from -6 to 6
- key_input: bfloat16 [16, 1024, 1024], P(('inner', 'outer'), 'head'), may hold values from -6 to 6
- value_input: bfloat16 [16, 1024, 1024], P(('inner', 'outer'), 'head'), may hold values from -6 to 6
- outputs: bfloat16 [16, 1024, 2048], P(('inner', 'outer'), 'head'), may hold values from -6 to 6
- output_gradient: bfloat16 [16, 1024, 2048], P(('inner', 'outer'), 'head'), may hold values from -6 to 6
- log_sum_exp: float32 [16, 1024, 16], P(('inner', 'outer'), 'head'), may hold values from -1 to 16
- block_order: int32 [32], replicated, may hold values from 0 to 31, as said below
Outputs:
- query_grad: bfloat16 [16, 1024, 2048], P(('inner', 'outer'), 'head')
- key_gradient: bfloat16 [16, 1024, 1024], P(('inner', 'outer'), 'head')
- value_gradient: bfloat16 [16, 1024, 1024], P(('inner', 'outer'), 'head')
The draws below stay inside these ranges and needn't reach their ends.
Inputs may be any that keep to these rules, and one draw needn't show every extreme that they name: `block_order`: A permutation of the 32 sequence blocks in which storage blocks 2 c and 2 c + 1 hold blocks b and 31 - b for some b below 16.
All inputs are finite; a program needn't handle non-finite values.
Results may differ from the reference program's by a relative error of at most 0.0052.
Values may be sent and summed in bfloat16 or wider, within the bound.
A program may use at most 64 MiB of HBM per device.

```python
import math
import jax
import jax.numpy as jnp
from jax import lax

QUERY_HEADS = 16
KEY_VALUE_HEADS = 8
HEAD_SIZE = 128
CONTEXT_ROWS = 1024
BLK = 512
CONTEXT_GROUPS = 16


def paired_order(key):
    firsts = jax.random.permutation(key, CONTEXT_GROUPS).astype(jnp.int32)
    seconds = (2 * CONTEXT_GROUPS - 1 - firsts).astype(jnp.int32)
    return jnp.stack([firsts, seconds], axis=1).reshape(2 * CONTEXT_GROUPS)


def draw_block_order(key, part):
    return paired_order(key)


def draw_log_sum_exp(key, part):
    ordering = paired_order(key)
    key = jax.random.fold_in(key, 11)
    row_ids = jnp.arange(CONTEXT_GROUPS * CONTEXT_ROWS, dtype=jnp.int32)
    places = ordering[row_ids // BLK] * BLK + row_ids % BLK
    baseline = jnp.log(places.astype(jnp.float32) + 1.0) + 0.5
    jitter = jnp.clip(0.4 * jax.random.normal(key, (CONTEXT_GROUPS * CONTEXT_ROWS, QUERY_HEADS), jnp.float32), -1.0, 1.0)
    return (baseline[:, None] + jitter).reshape(CONTEXT_GROUPS, CONTEXT_ROWS, QUERY_HEADS)


def shard_levels(key, shape, pieces, least, high):
    gain, own = 1.0, jax.random.fold_in(key, 6)
    for dim, blocks in pieces:
        draws = jnp.exp(jax.random.uniform(jax.random.fold_in(own, dim), (blocks,), jnp.float32, least / len(pieces), high / len(pieces)))
        gain = gain * jnp.repeat(draws, shape[dim] // blocks).reshape([-1 if axis == dim else 1 for axis in range(len(shape))])
    return gain


def gaussian(key, dims, spread, reach, pieces=(), held_as=jnp.bfloat16):
    array = spread * jax.random.normal(key, dims, jnp.float32)
    if pieces:
        array = array * shard_levels(key, dims, pieces, -0.22, 0.18)
    return jnp.clip(array, -reach, reach).astype(held_as)


def setup_inputs(seed: int = 0) -> dict:
    streams_of = jax.random.split(jax.random.key(seed), 8)
    queries = gaussian(streams_of[0], (CONTEXT_GROUPS, CONTEXT_ROWS, QUERY_HEADS * HEAD_SIZE), 1.0, 6.0, ((0, 16), (1, 8)))
    key_input = gaussian(streams_of[1], (CONTEXT_GROUPS, CONTEXT_ROWS, KEY_VALUE_HEADS * HEAD_SIZE), 1.0, 6.0, ((0, 16), (1, 8)))
    value_input = gaussian(streams_of[2], (CONTEXT_GROUPS, CONTEXT_ROWS, KEY_VALUE_HEADS * HEAD_SIZE), 1.0, 6.0, ((0, 16), (1, 8)))
    outputs = gaussian(streams_of[3], (CONTEXT_GROUPS, CONTEXT_ROWS, QUERY_HEADS * HEAD_SIZE), 1.0, 6.0, ((0, 16), (1, 8)))
    output_gradient = gaussian(streams_of[4], (CONTEXT_GROUPS, CONTEXT_ROWS, QUERY_HEADS * HEAD_SIZE), 1.0, 6.0, ((0, 16), (1, 8)))
    log_sum_exp = draw_log_sum_exp(jax.random.fold_in(streams_of[7], 71), 0)
    block_order = draw_block_order(jax.random.fold_in(streams_of[7], 71), 0)
    return {"queries": queries, "key_input": key_input, "value_input": value_input, "outputs": outputs, "output_gradient": output_gradient, "log_sum_exp": log_sum_exp, "block_order": block_order}


def reference(queries, key_input, value_input, outputs, output_gradient, log_sum_exp, block_order):
    sequence_length = CONTEXT_GROUPS * CONTEXT_ROWS
    heads_per_group = QUERY_HEADS // KEY_VALUE_HEADS
    score_scale = HEAD_SIZE ** -0.5
    row_ids = jnp.arange(sequence_length, dtype=jnp.int32)
    positions = (block_order[row_ids // BLK] * BLK + row_ids % BLK).astype(jnp.int32)
    query_gathered = queries.reshape(sequence_length, KEY_VALUE_HEADS, heads_per_group, HEAD_SIZE).astype(jnp.float32)
    keys_gathered = key_input.reshape(sequence_length, KEY_VALUE_HEADS, HEAD_SIZE).astype(jnp.float32)
    values_gathered = value_input.reshape(sequence_length, KEY_VALUE_HEADS, HEAD_SIZE).astype(jnp.float32)
    gradient_gathered = output_gradient.reshape(sequence_length, KEY_VALUE_HEADS, heads_per_group, HEAD_SIZE).astype(jnp.float32)
    output_gathered = outputs.reshape(sequence_length, KEY_VALUE_HEADS, heads_per_group, HEAD_SIZE).astype(jnp.float32)
    row_delta = jnp.sum(gradient_gathered * output_gathered, axis=3)
    log_normalizer = log_sum_exp.reshape(sequence_length, KEY_VALUE_HEADS, heads_per_group)
    width = math.gcd(CONTEXT_ROWS, 256)

    def visit(carried, block_index):
        key_gradient_total, value_gradient_total = carried
        start = (block_index * width).astype(jnp.int32)
        query_block = lax.dynamic_slice_in_dim(query_gathered, start, width, 0)
        grad_block = lax.dynamic_slice_in_dim(gradient_gathered, start, width, 0)
        norm_block = jnp.transpose(lax.dynamic_slice_in_dim(log_normalizer, start, width, 0), (1, 2, 0))
        delta_block = jnp.transpose(lax.dynamic_slice_in_dim(row_delta, start, width, 0), (1, 2, 0))
        place_block = lax.dynamic_slice_in_dim(positions, start, width, 0)
        scores = jnp.einsum("qhgd,khd->hgqk", query_block, keys_gathered) * score_scale
        visible = positions[None, :] <= place_block[:, None]
        probs = jnp.where(visible, jnp.exp(scores - norm_block[..., None]), 0.0)
        prob_grad = jnp.einsum("qhgd,khd->hgqk", grad_block, values_gathered)
        score_grad = lax.optimization_barrier((probs * (prob_grad - delta_block[..., None])).astype(jnp.bfloat16)).astype(jnp.float32)
        probs_low = lax.optimization_barrier(probs.astype(jnp.bfloat16)).astype(jnp.float32)
        query_part = jnp.einsum("hgqk,khd->qhgd", score_grad, keys_gathered) * score_scale
        key_gradient_total = key_gradient_total + jnp.einsum("hgqk,qhgd->khd", score_grad, query_block)
        value_gradient_total = value_gradient_total + jnp.einsum("hgqk,qhgd->khd", probs_low, grad_block)
        return (key_gradient_total, value_gradient_total), query_part.astype(jnp.bfloat16)

    empty_key_value = jnp.zeros((sequence_length, KEY_VALUE_HEADS, HEAD_SIZE), jnp.float32)
    steps_count = sequence_length // width
    (key_gradient_total, value_gradient_total), query_parts = lax.scan(visit, (empty_key_value, empty_key_value), jnp.arange(steps_count, dtype=jnp.int32))
    query_grad = query_parts.reshape(CONTEXT_GROUPS, CONTEXT_ROWS, QUERY_HEADS * HEAD_SIZE)
    key_gradient = (key_gradient_total * score_scale).astype(jnp.bfloat16).reshape(CONTEXT_GROUPS, CONTEXT_ROWS, KEY_VALUE_HEADS * HEAD_SIZE)
    value_gradient = value_gradient_total.astype(jnp.bfloat16).reshape(CONTEXT_GROUPS, CONTEXT_ROWS, KEY_VALUE_HEADS * HEAD_SIZE)
    return (query_grad, key_gradient, value_gradient)
```

```python
import functools

import jax
import jax.numpy as jnp
from jax import lax
from jax.experimental import pallas as pl
from jax.experimental.pallas import tpu as pltpu
from jax.sharding import PartitionSpec as P

MESH = pl.DeviceIdType.MESH
F32, BF16 = jnp.float32, jnp.bfloat16
HEAD = 128
HEADS = 8
PART = 128
HALF = 512
ROWS = 1024
LOG2E = 1.4426950408889634
SCALE = HEAD**-0.5
TILE = 256
NT = (((1,), (1,)), ((), ()))


def remote(src, dst, send_sem, recv_sem, device):
    return pltpu.make_async_remote_copy(
        src_ref=src,
        dst_ref=dst,
        send_sem=send_sem,
        recv_sem=recv_sem,
        device_id=device,
        device_id_type=MESH,
    )


def dot(a, b):
    return jnp.dot(a, b, preferred_element_type=F32)


def dot_nt(a, b):
    return lax.dot_general(a, b, NT, preferred_element_type=F32)


def block(q, do, stats, k, v, mask):
    k_t = k.T
    dk = dv = None
    dq = []
    for e in range(2):
        for t in range(HALF // TILE):
            cols = slice(t * TILE, (t + 1) * TILE)
            q_e = q[cols, e * HEAD : (e + 1) * HEAD]
            do_e = do[cols, e * HEAD : (e + 1) * HEAD]
            scores = dot_nt(k, q_e)
            probs = jnp.exp2(scores * (SCALE * LOG2E) - stats[e : e + 1, cols])
            if mask:
                key_id = lax.broadcasted_iota(jnp.int32, (HALF, TILE), 0)
                query_id = lax.broadcasted_iota(jnp.int32, (HALF, TILE), 1) + t * TILE
                probs = jnp.where(key_id <= query_id, probs, 0.0)
            prob_grad = dot_nt(v, do_e)
            score_grad = (probs * (prob_grad - stats[2 + e : 3 + e, cols])).astype(BF16)
            dv_e = dot(probs.astype(BF16), do_e)
            dk_e = dot(score_grad, q_e)
            dv = dv_e if dv is None else dv + dv_e
            dk = dk_e if dk is None else dk + dk_e
            dq.append((e, t, dot(k_t, score_grad)))
    return dq, dk, dv


def kernel(
    order,
    q_in,
    k_in,
    v_in,
    o_in,
    do_in,
    lse_in,
    dq_out,
    dk_out,
    dv_out,
    o_vm,
    do_vm,
    stat_send,
    QD,
    KV,
    ST,
    DQ,
    DKV,
    dq_send,
    dq_recv,
    core_recv,
    far_send,
    far_recv,
    dq_fin,
    dkv_fin,
    s_loc,
    s_a2a,
    r_a2a,
    s_q,
    r_q,
    s_k,
    r_k,
    s_dq,
    r_dq,
    s_dk,
    r_dk,
    s_out,
    r_out,
):
    head, inner, outer = lax.axis_index("head"), lax.axis_index("inner"), lax.axis_index("outer")
    x_lo, z = head // 4, head % 4
    x_hi, core = outer // 2, outer % 2

    def peer(r):
        return ((x_lo + r // 4) % 2) * 4 + (z + r % 4) % 4

    q_dev = {
        1: (head, (inner + 1) % 4, outer),
        2: (head, (inner + 3) % 4, outer),
        3: (head, (inner + 2) % 4, outer),
    }
    back_dev = {1: q_dev[2], 2: q_dev[1], 3: q_dev[3]}
    core_dev = (head, inner, x_hi * 2 + (core + 1) % 2)
    far_dev = (head, inner, ((x_hi + 1) % 2) * 2 + core)

    barrier = pltpu.get_barrier_semaphore()
    everyone = [(peer(r), inner, outer) for r in range(1, 8)] + [q_dev[1], q_dev[2], q_dev[3], core_dev, far_dev]
    for device in everyone:
        pl.semaphore_signal(barrier, inc=1, device_id=device, device_id_type=MESH)

    mine = pl.ds(pl.multiple_of(head * PART, PART), PART)

    def wide(p, n):
        return pl.ds(pl.multiple_of(p * n, n), n)

    local = [
        pltpu.make_async_copy(o_in.at[0], o_vm, s_loc.at[0]),
        pltpu.make_async_copy(do_in.at[0], do_vm, s_loc.at[1]),
        pltpu.make_async_copy(q_in.at[0, :, wide(head, 256)], QD.at[0, 0, mine], s_loc.at[2]),
        pltpu.make_async_copy(do_in.at[0, :, wide(head, 256)], QD.at[0, 1, mine], s_loc.at[3]),
        pltpu.make_async_copy(k_in.at[0, :, wide(head, 128)], KV.at[0, 0, mine], s_loc.at[4]),
        pltpu.make_async_copy(v_in.at[0, :, wide(head, 128)], KV.at[0, 1, mine], s_loc.at[5]),
    ]
    for copy in local:
        copy.start()
    pl.semaphore_wait(barrier, len(everyone))

    def exchange(i, r):
        p = peer(r)
        src, dst = [
            (k_in.at[0, :, wide(p, 128)], KV.at[0, 0, mine]),
            (v_in.at[0, :, wide(p, 128)], KV.at[0, 1, mine]),
            (q_in.at[0, :, wide(p, 256)], QD.at[0, 0, mine]),
            (do_in.at[0, :, wide(p, 256)], QD.at[0, 1, mine]),
            (stat_send.at[p], ST.at[0, :, mine]),
        ][i]
        return remote(src, dst, s_a2a.at[i, r], r_a2a.at[i, r], (p, inner, outer))

    for r in range(1, 8):
        for i in range(4):
            exchange(i, r).start()

    local[0].wait()
    local[1].wait()
    lane = lax.broadcasted_iota(jnp.int32, (PART, 128), 1)
    delta = jnp.zeros((PART, 128), F32)
    for h in range(2 * HEADS):
        cols = slice(h * HEAD, (h + 1) * HEAD)
        total = jnp.sum(o_vm[:, cols].astype(F32) * do_vm[:, cols].astype(F32), axis=1, keepdims=True)
        delta = jnp.where(lane == h, total, delta)
    delta_t = delta.T
    lse_t = (lse_in[0] * LOG2E).T
    stat_send[...] = jnp.zeros(stat_send.shape, F32)
    for g in range(HEADS):
        stat_send[g, 0:2, :] = lse_t[2 * g : 2 * g + 2, :]
        stat_send[g, 2:4, :] = delta_t[2 * g : 2 * g + 2, :]
    own_stat = pltpu.make_async_copy(stat_send.at[head], ST.at[0, :, mine], s_loc.at[6])
    own_stat.start()
    for r in range(1, 8):
        exchange(4, r).start()

    def clear(i, _):
        for s in range(4):
            DQ[s, pl.ds(pl.multiple_of(i * 32, 32), 32), :] = jnp.zeros((32, ROWS), F32)
            for j in range(2):
                DKV[s, j, pl.ds(pl.multiple_of(i * 128, 128), 128), :] = jnp.zeros((128, HEAD), F32)
        return 0

    lax.fori_loop(0, 8, clear, 0)

    first = pl.multiple_of(x_lo * HALF, HALF)
    second = pl.multiple_of(HALF - x_lo * HALF, HALF)
    starts = (first, second)

    def send_q(slot, part):
        if part == 2:
            src, dst = ST.at[0], ST.at[slot]
        else:
            rows = pl.ds(starts[part], HALF)
            src, dst = QD.at[0, :, rows], QD.at[slot, :, rows]
        return remote(src, dst, s_q.at[slot, part], r_q.at[slot, part], q_dev[slot])

    def send_k(slot, part):
        rows = pl.ds(starts[part], HALF)
        src = KV.at[2 if slot == 3 else 0, :, rows]
        device = far_dev if slot == 2 else core_dev
        return remote(src, KV.at[slot, :, rows], s_k.at[slot, part], r_k.at[slot, part], device)

    def add_block(qs, q_lo, ks, k_lo, mask):
        q_rows, k_rows = pl.ds(q_lo, HALF), pl.ds(k_lo, HALF)
        dq, dk, dv = block(
            QD[qs, 0, q_rows, :],
            QD[qs, 1, q_rows, :],
            ST[qs, :, q_rows],
            KV[ks, 0, k_rows, :],
            KV[ks, 1, k_rows, :],
            mask,
        )
        for e, t, part in dq:
            DQ[qs, e * HEAD : (e + 1) * HEAD, pl.ds(pl.multiple_of(q_lo + t * TILE, TILE), TILE)] += part
        DKV[ks, 0, k_rows, :] += dk
        DKV[ks, 1, k_rows, :] += dv

    for copy in local[2:]:
        copy.wait()
    own_stat.wait()
    for r in (1, 2, 3):
        for i in range(5):
            exchange(i, r).wait_recv()
    for copy in (send_k(2, 0), send_k(1, 0), send_q(1, 0), send_q(2, 0)):
        copy.start()
    for r in (4, 5, 6, 7):
        for i in range(5):
            exchange(i, r).wait_recv()
    for copy in (send_k(2, 1), send_k(1, 1), send_q(1, 1), send_q(2, 1)):
        copy.start()
    for slot, part in ((1, 2), (2, 2), (3, 0), (3, 1), (3, 2)):
        send_q(slot, part).start()

    def own_diagonal(i, _):
        at = pl.multiple_of(i * HALF, HALF)
        add_block(0, at, 0, at, True)
        return 0

    lax.fori_loop(0, 2, own_diagonal, 0)
    add_block(0, HALF, 0, 0, False)

    def return_dq(slot):
        return remote(dq_send.at[slot - 1], dq_recv.at[slot - 1], s_dq.at[slot], r_dq.at[slot], back_dev[slot])

    def return_core(slot):
        return remote(DKV.at[slot], core_recv.at[slot // 2], s_dk.at[slot], r_dk.at[slot], core_dev)

    def return_far():
        return remote(far_send, far_recv, s_dk.at[2], r_dk.at[2], far_dev)

    def pack_dq(slot):
        def step(i, _):
            rows = pl.ds(pl.multiple_of(i * 32, 32), 32)
            dq_send[slot - 1, rows, :] = DQ[slot, rows, :].astype(BF16)
            return 0

        lax.fori_loop(0, 8, step, 0)
        return_dq(slot).start()

    def pair(n, _):
        q_step, r = n // 4, n % 4
        later = (q_step + 3) // 4
        qs = q_step
        ks = r + later * (3 - 2 * r)

        for slot in (1, 2, 3):

            @pl.when(n == slot)
            def _():
                for part in range(2):
                    send_k(slot, part).wait_recv()
                if slot == 2:
                    for part in range(2):
                        send_k(3, part).start()

            @pl.when(n == 4 * slot)
            def _():
                for part in range(3):
                    send_q(slot, part).wait_recv()

        q_inner = (inner + (qs + 1) // 2 + 2 * ((qs % 2) * (1 - qs // 2))) % 4
        k_outer = ((x_hi + ks // 2) % 2) * 2 + (core + ks % 2) % 2
        sel = order[2 * (inner * 4 + k_outer)] < order[2 * (q_inner * 4 + outer)]
        add_block(qs, HALF, ks, 0, False)

        def pick(lo, hi):
            return jnp.where(sel, lo, hi)

        dq, dk, dv = block(
            pick(QD[qs, 0, 0:HALF, :], QD[qs, 0, HALF:ROWS, :]),
            pick(QD[qs, 1, 0:HALF, :], QD[qs, 1, HALF:ROWS, :]),
            pick(ST[qs, :, 0:HALF], ST[qs, :, HALF:ROWS]),
            pick(KV[ks, 0, 0:HALF, :], KV[ks, 0, HALF:ROWS, :]),
            pick(KV[ks, 1, 0:HALF, :], KV[ks, 1, HALF:ROWS, :]),
            False,
        )
        for e, t, part in dq:
            zero = jnp.zeros_like(part)
            rows = slice(e * HEAD, (e + 1) * HEAD)
            DQ[qs, rows, t * TILE : (t + 1) * TILE] += jnp.where(sel, part, zero)
            DQ[qs, rows, HALF + t * TILE : HALF + (t + 1) * TILE] += jnp.where(sel, zero, part)
        for j, part in enumerate((dk, dv)):
            zero = jnp.zeros_like(part)
            DKV[ks, j, 0:HALF, :] += jnp.where(sel, part, zero)
            DKV[ks, j, HALF:ROWS, :] += jnp.where(sel, zero, part)

        for slot in (1, 2, 3):

            @pl.when(n == 4 * slot + 3)
            def _():
                pack_dq(slot)

        for slot, at in ((3, 12), (1, 14)):

            @pl.when(n == at)
            def _():
                return_core(slot).start()

        @pl.when(n == 13)
        def _():
            return_core(3).wait_recv()

            def step(i, _):
                rows = pl.ds(pl.multiple_of(i * 128, 128), 128)
                for j in range(2):
                    far_send[j, rows, :] = (DKV[2, j, rows, :] + core_recv[1, j, rows, :]).astype(BF16)
                return 0

            lax.fori_loop(0, 8, step, 0)
            return_far().start()

        return 0

    lax.fori_loop(1, 16, pair, 0)

    def give(kind, r):
        p = peer(r)
        rows = wide(p, PART)
        if kind == 0:
            src, dst = dq_fin.at[rows], dq_out.at[0, :, wide(head, 256)]
        elif kind == 1:
            src, dst = dkv_fin.at[0, rows], dk_out.at[0, :, wide(head, 128)]
        else:
            src, dst = dkv_fin.at[1, rows], dv_out.at[0, :, wide(head, 128)]
        if r == 0:
            return pltpu.make_async_copy(src, dst, s_out.at[kind, 0])
        return remote(src, dst, s_out.at[kind, r], r_out.at[kind, r], (p, inner, outer))

    return_core(1).wait_recv()
    return_far().wait_recv()
    for r in (4, 5, 6, 7, 1, 2, 3, 0):
        rows = wide(peer(r), PART)
        for j, scale in ((0, SCALE), (1, 1.0)):
            total = DKV[0, j, rows, :] + core_recv[0, j, rows, :] + far_recv[j, rows, :].astype(F32)
            dkv_fin[j, rows, :] = (total * scale).astype(BF16)
        give(1, r).start()
        give(2, r).start()
    for slot in (1, 2, 3):
        return_dq(slot).wait_recv()
    for r in (4, 5, 6, 7, 1, 2, 3, 0):
        rows = wide(peer(r), PART)
        for e in range(2):
            feats = slice(e * HEAD, (e + 1) * HEAD)
            total = DQ[0, feats, rows]
            for slot in range(3):
                total = total + dq_recv[slot, feats, rows].astype(F32)
            dq_fin[rows, feats] = (total * SCALE).T.astype(BF16)
        give(0, r).start()

    for r in range(1, 8):
        for i in range(5):
            exchange(i, r).wait_send()
    for slot in (1, 2, 3):
        for part in range(3):
            send_q(slot, part).wait_send()
        for part in range(2):
            send_k(slot, part).wait_send()
        return_dq(slot).wait_send()
    for slot in (1, 3):
        return_core(slot).wait_send()
    return_far().wait_send()
    for kind in range(3):
        for r in range(8):
            give(kind, r).wait()


def per_device(queries, key_input, value_input, outputs, output_gradient, log_sum_exp, block_order):
    any_space = pl.BlockSpec(memory_space=pl.ANY)
    dma = pltpu.SemaphoreType.DMA
    return pl.pallas_call(
        kernel,
        out_shape=(
            jax.ShapeDtypeStruct((1, PART, 2048), BF16),
            jax.ShapeDtypeStruct((1, PART, 1024), BF16),
            jax.ShapeDtypeStruct((1, PART, 1024), BF16),
        ),
        in_specs=[pl.BlockSpec(memory_space=pltpu.SMEM)]
        + [any_space] * 5
        + [pl.BlockSpec(memory_space=pltpu.VMEM)],
        out_specs=(any_space,) * 3,
        scratch_shapes=[
            pltpu.VMEM((PART, 2048), BF16),
            pltpu.VMEM((PART, 2048), BF16),
            pltpu.VMEM((HEADS, 8, PART), F32),
            pltpu.VMEM((4, 2, ROWS, 256), BF16),
            pltpu.VMEM((4, 2, ROWS, HEAD), BF16),
            pltpu.VMEM((4, 8, ROWS), F32),
            pltpu.VMEM((4, 256, ROWS), F32),
            pltpu.VMEM((4, 2, ROWS, HEAD), F32),
            pltpu.VMEM((3, 256, ROWS), BF16),
            pltpu.VMEM((3, 256, ROWS), BF16),
            pltpu.VMEM((2, 2, ROWS, HEAD), F32),
            pltpu.VMEM((2, ROWS, HEAD), BF16),
            pltpu.VMEM((2, ROWS, HEAD), BF16),
            pltpu.VMEM((ROWS, 256), BF16),
            pltpu.VMEM((2, ROWS, HEAD), BF16),
            dma((8,)),
            dma((5, 8)),
            dma((5, 8)),
            dma((4, 3)),
            dma((4, 3)),
            dma((4, 2)),
            dma((4, 2)),
            dma((4,)),
            dma((4,)),
            dma((4,)),
            dma((4,)),
            dma((3, 8)),
            dma((3, 8)),
        ],
        compiler_params=pltpu.CompilerParams(
            collective_id=0, has_side_effects=True, vmem_limit_bytes=56 * 1024 * 1024
        ),
        name="attention_backward",
    )(block_order, queries, key_input, value_input, outputs, output_gradient, log_sum_exp)


def solution(mesh):
    split = P(("inner", "outer"), "head", None)
    return jax.shard_map(
        per_device, mesh=mesh, in_specs=(split,) * 6 + (P(),), out_specs=(split,) * 3, check_vma=False
    )
```

```python
import functools

import jax
import jax.numpy as jnp
from jax import lax
from jax.experimental import pallas as pl
from jax.experimental.pallas import tpu as pltpu
from jax.sharding import PartitionSpec as P

MESH = pl.DeviceIdType.MESH
F32, BF16 = jnp.float32, jnp.bfloat16
HEAD = 128
HEADS = 8
PART = 128
HALF = 512
ROWS = 1024
LOG2E = 1.4426950408889634
SCALE = HEAD**-0.5
TILE = 256
NT = (((1,), (1,)), ((), ()))


def remote(src, dst, send_sem, recv_sem, device):
    return pltpu.make_async_remote_copy(
        src_ref=src,
        dst_ref=dst,
        send_sem=send_sem,
        recv_sem=recv_sem,
        device_id=device,
        device_id_type=MESH,
    )


def dot(a, b):
    return jnp.dot(a, b, preferred_element_type=F32)


def dot_nt(a, b):
    return lax.dot_general(a, b, NT, preferred_element_type=F32)


def block(q, do, stats, k, v, mask, heads=(0, 1)):
    k_t = k.T
    dk = dv = None
    dq = []
    for e in heads:
        for t in range(HALF // TILE):
            cols = slice(t * TILE, (t + 1) * TILE)
            q_e = q[cols, e * HEAD : (e + 1) * HEAD]
            do_e = do[cols, e * HEAD : (e + 1) * HEAD]
            scores = dot_nt(k, q_e)
            probs = jnp.exp2(scores * (SCALE * LOG2E) - stats[e : e + 1, cols])
            if mask:
                key_id = lax.broadcasted_iota(jnp.int32, (HALF, TILE), 0)
                query_id = lax.broadcasted_iota(jnp.int32, (HALF, TILE), 1) + t * TILE
                probs = jnp.where(key_id <= query_id, probs, 0.0)
            prob_grad = dot_nt(v, do_e)
            score_grad = (probs * (prob_grad - stats[2 + e : 3 + e, cols])).astype(BF16)
            dv_e = dot(probs.astype(BF16), do_e)
            dk_e = dot(score_grad, q_e)
            dv = dv_e if dv is None else dv + dv_e
            dk = dk_e if dk is None else dk + dk_e
            dq.append((e, t, dot(k_t, score_grad)))
    return dq, dk, dv


def kernel(
    order,
    q_in,
    k_in,
    v_in,
    o_in,
    do_in,
    lse_in,
    dq_out,
    dk_out,
    dv_out,
    o_vm,
    do_vm,
    qd_send,
    kv_send,
    stat_send,
    QD,
    KV,
    ST,
    DQ,
    DKV,
    dq_send,
    dq_recv,
    core_recv,
    far_send,
    far_recv,
    dq_fin,
    dkv_fin,
    s_loc,
    s_a2a,
    r_a2a,
    s_q,
    r_q,
    s_k,
    r_k,
    s_dq,
    r_dq,
    s_dk,
    r_dk,
    s_out,
    r_out,
):
    head, inner, outer = lax.axis_index("head"), lax.axis_index("inner"), lax.axis_index("outer")
    x_lo, z = head // 4, head % 4
    x_hi, core = outer // 2, outer % 2

    def peer(r):
        return ((x_lo + r // 4) % 2) * 4 + (z + r % 4) % 4

    q_dev = {
        1: (head, (inner + 1) % 4, outer),
        2: (head, (inner + 3) % 4, outer),
        3: (head, (inner + 2) % 4, outer),
    }
    back_dev = {1: q_dev[2], 2: q_dev[1], 3: q_dev[3]}
    core_dev = (head, inner, x_hi * 2 + (core + 1) % 2)
    far_dev = (head, inner, ((x_hi + 1) % 2) * 2 + core)

    barrier = pltpu.get_barrier_semaphore()
    everyone = [(peer(r), inner, outer) for r in range(1, 8)] + [q_dev[1], q_dev[2], q_dev[3], core_dev, far_dev]
    for device in everyone:
        pl.semaphore_signal(barrier, inc=1, device_id=device, device_id_type=MESH)

    mine = pl.ds(pl.multiple_of(head * PART, PART), PART)

    def wide(p, n):
        return pl.ds(pl.multiple_of(p * n, n), n)

    def fetch(r, i):
        p = peer(r)
        src = (q_in, do_in, k_in, v_in)[i].at[0, :, wide(p, (256, 256, 128, 128)[i])]
        if r == 0:
            dst = (QD if i < 2 else KV).at[0, i % 2, mine]
        else:
            dst = (qd_send if i < 2 else kv_send).at[r, i % 2]
        return pltpu.make_async_copy(src, dst, s_loc.at[i, r])

    def exchange(i, r):
        p = peer(r)
        src, dst = [
            (qd_send.at[r], QD.at[0, :, mine]),
            (kv_send.at[r], KV.at[0, :, mine]),
            (stat_send.at[p], ST.at[0, :, mine]),
        ][i]
        return remote(src, dst, s_a2a.at[i, r], r_a2a.at[i, r], (p, inner, outer))

    turn = (4, 1, 5, 3, 7, 2, 6)
    for r in turn:
        for i in range(4):
            fetch(r, i).start()
    rows_in = [
        pltpu.make_async_copy(o_in.at[0], o_vm, s_loc.at[4, 0]),
        pltpu.make_async_copy(do_in.at[0], do_vm, s_loc.at[4, 1]),
    ]
    for copy in rows_in:
        copy.start()
    for i in range(4):
        fetch(0, i).start()
    pl.semaphore_wait(barrier, len(everyone))
    for r in turn:
        for i in range(4):
            fetch(r, i).wait()
        exchange(0, r).start()
        exchange(1, r).start()

    for copy in rows_in:
        copy.wait()
    lane = lax.broadcasted_iota(jnp.int32, (PART, 128), 1)
    delta = jnp.zeros((PART, 128), F32)
    for h in range(2 * HEADS):
        cols = slice(h * HEAD, (h + 1) * HEAD)
        total = jnp.sum(o_vm[:, cols].astype(F32) * do_vm[:, cols].astype(F32), axis=1, keepdims=True)
        delta = jnp.where(lane == h, total, delta)
    delta_t = delta.T
    lse_t = lse_in[0] * LOG2E
    stat_send[...] = jnp.zeros(stat_send.shape, F32)
    for g in range(HEADS):
        stat_send[g, 0:2, :] = lse_t[2 * g : 2 * g + 2, :]
        stat_send[g, 2:4, :] = delta_t[2 * g : 2 * g + 2, :]
    own_stat = pltpu.make_async_copy(stat_send.at[head], ST.at[0, :, mine], s_loc.at[4, 2])
    own_stat.start()
    for r in range(1, 8):
        exchange(2, r).start()

    def clear(i, _):
        for s in range(4):
            DQ[s, pl.ds(pl.multiple_of(i * 32, 32), 32), :] = jnp.zeros((32, ROWS), F32)
            for j in range(2):
                DKV[s, j, pl.ds(pl.multiple_of(i * 128, 128), 128), :] = jnp.zeros((128, HEAD), F32)
        return 0

    lax.fori_loop(0, 8, clear, 0)

    LO, HI = 0, 1

    def half(part):
        return pl.ds(part * HALF, HALF)

    def send_q(slot, part, what):
        rows = half(part)
        if what == "stats":
            src, dst = ST.at[0, :, rows], ST.at[slot, :, rows]
            return remote(src, dst, s_q.at[slot, part, 2], r_q.at[slot, part, 2], q_dev[slot])
        if slot < 3:
            src, dst = QD.at[0, :, rows], QD.at[slot, :, rows]
            return remote(src, dst, s_q.at[slot, part, 0], r_q.at[slot, part, 0], q_dev[slot])
        src, dst = QD.at[2 - what, what, rows], QD.at[3, what, rows]
        return remote(src, dst, s_q.at[3, part, what], r_q.at[3, part, what], q_dev[2 - what])

    def send_k(slot, part):
        rows = half(part)
        src = KV.at[2 if slot == 3 else 0, :, rows]
        device = far_dev if slot == 2 else core_dev
        return remote(src, KV.at[slot, :, rows], s_k.at[slot, part], r_k.at[slot, part], device)

    def add_block(qs, q_lo, ks, k_lo, mask, heads=(0, 1)):
        q_rows, k_rows = pl.ds(q_lo, HALF), pl.ds(k_lo, HALF)
        dq, dk, dv = block(
            QD[qs, 0, q_rows, :],
            QD[qs, 1, q_rows, :],
            ST[qs, :, q_rows],
            KV[ks, 0, k_rows, :],
            KV[ks, 1, k_rows, :],
            mask,
            heads,
        )
        for e, t, part in dq:
            DQ[qs, e * HEAD : (e + 1) * HEAD, pl.ds(pl.multiple_of(q_lo + t * TILE, TILE), TILE)] += part
        DKV[ks, 0, k_rows, :] += dk
        DKV[ks, 1, k_rows, :] += dv

    def add_either(qs, ks, heads=(0, 1)):
        q_inner = (inner + (qs + 1) // 2 + 2 * ((qs % 2) * (1 - qs // 2))) % 4
        k_outer = ((x_hi + ks // 2) % 2) * 2 + (core + ks % 2) % 2
        sel = order[2 * (inner * 4 + k_outer)] < order[2 * (q_inner * 4 + outer)]

        def pick(lo, hi):
            return jnp.where(sel, lo, hi)

        dq, dk, dv = block(
            pick(QD[qs, 0, 0:HALF, :], QD[qs, 0, HALF:ROWS, :]),
            pick(QD[qs, 1, 0:HALF, :], QD[qs, 1, HALF:ROWS, :]),
            pick(ST[qs, :, 0:HALF], ST[qs, :, HALF:ROWS]),
            pick(KV[ks, 0, 0:HALF, :], KV[ks, 0, HALF:ROWS, :]),
            pick(KV[ks, 1, 0:HALF, :], KV[ks, 1, HALF:ROWS, :]),
            False,
            heads,
        )
        for e, t, part in dq:
            zero = jnp.zeros_like(part)
            rows = slice(e * HEAD, (e + 1) * HEAD)
            DQ[qs, rows, t * TILE : (t + 1) * TILE] += jnp.where(sel, part, zero)
            DQ[qs, rows, HALF + t * TILE : HALF + (t + 1) * TILE] += jnp.where(sel, zero, part)
        for j, part in enumerate((dk, dv)):
            zero = jnp.zeros_like(part)
            DKV[ks, j, 0:HALF, :] += jnp.where(sel, part, zero)
            DKV[ks, j, HALF:ROWS, :] += jnp.where(sel, zero, part)

    def add_full(qs, ks, heads=(0, 1)):
        add_block(qs, HALF, ks, 0, False, heads)

    for i in range(4):
        fetch(0, i).wait()
    own_stat.wait()
    for part in (HI, LO):
        base = 4 * ((1 - x_lo) if part == HI else x_lo)
        for j in range(4):

            def arrived(r=base + j):
                for i in range(3):
                    exchange(i, r).wait_recv()

            if j == 0:
                pl.when(base > 0)(arrived)
            else:
                arrived()
        for slot in (2, 1):
            send_k(slot, part).start()
        for slot in (1, 2):
            send_q(slot, part, "stats").start()
            send_q(slot, part, 0).start()
    for part in (HI, LO):
        send_q(3, part, "stats").start()

    def own_diagonal(i, _):
        at = pl.multiple_of(i * HALF, HALF)
        add_block(0, at, 0, at, True)
        return 0

    lax.fori_loop(0, 2, own_diagonal, 0)
    add_block(0, HALF, 0, 0, False)

    def return_dq(slot, e):
        feats = pl.ds(e * HEAD, HEAD)
        src, dst = dq_send.at[slot - 1, feats], dq_recv.at[slot - 1, feats]
        return remote(src, dst, s_dq.at[slot, e], r_dq.at[slot, e], back_dev[slot])

    def return_core(slot):
        return remote(DKV.at[slot], core_recv.at[slot // 2], s_dk.at[slot], r_dk.at[slot], core_dev)

    def return_far():
        return remote(far_send, far_recv, s_dk.at[2], r_dk.at[2], far_dev)

    def pack_dq(slot, e):
        def step(i, _):
            rows = pl.ds(pl.multiple_of(e * HEAD + i * 32, 32), 32)
            dq_send[slot - 1, rows, :] = DQ[slot, rows, :].astype(BF16)
            return 0

        lax.fori_loop(0, HEAD // 32, step, 0)
        return_dq(slot, e).start()

    def own_queries(ks, _):
        for slot in (1, 2, 3):

            @pl.when(ks == slot)
            def _():
                for part in range(2):
                    send_k(slot, part).wait_recv()
                if slot == 2:
                    for part in range(2):
                        send_k(3, part).start()

        add_full(0, ks)
        add_either(0, ks)
        return 0

    lax.fori_loop(1, 4, own_queries, 0)

    def arrive_and_forward(slot, part):
        send_q(slot, part, "stats").wait_recv()
        send_q(slot, part, 0).wait_recv()
        send_q(3, part, 2 - slot).start()

    def near_full(m, _):
        for slot in (1, 2):

            @pl.when(m == slot - 1)
            def _():
                arrive_and_forward(slot, HI)

        add_full(1 + m // 4, 3 - m % 4)
        return 0

    lax.fori_loop(0, 8, near_full, 0)

    def near_either(m, _):
        for slot in (1, 2):

            @pl.when(m == slot - 1)
            def _():
                arrive_and_forward(slot, LO)

        add_either(1 + m // 4, 3 - m % 4)
        for slot in (1, 2):

            @pl.when(m == 4 * slot - 1)
            def _():
                for e in range(2):
                    pack_dq(slot, e)

        return 0

    lax.fori_loop(0, 8, near_either, 0)

    for part in (HI, LO):
        for what in ("stats", 0, 1):
            send_q(3, part, what).wait_recv()

    def far_queries(m, _):
        ks = 3 - m
        add_full(3, ks)
        add_either(3, ks)

        @pl.when(m == 0)
        def _():
            return_core(3).start()

        return 0

    lax.fori_loop(0, 2, far_queries, 0)
    return_core(3).wait_recv()

    def pack_far(i, _):
        rows = pl.ds(pl.multiple_of(i * 128, 128), 128)
        for j in range(2):
            far_send[j, rows, :] = (DKV[2, j, rows, :] + core_recv[1, j, rows, :]).astype(BF16)
        return 0

    lax.fori_loop(0, 8, pack_far, 0)
    return_far().start()

    for e in range(2):

        def last_queries(m, _):
            ks = 1 - m
            add_full(3, ks, (e,))
            add_either(3, ks, (e,))
            if e == 1:

                @pl.when(m == 0)
                def _():
                    return_core(1).start()

            return 0

        lax.fori_loop(0, 2, last_queries, 0)
        pack_dq(3, e)

    def give(kind, r):
        p = peer(r)
        rows = wide(p, PART)
        if kind < 2:
            src = dq_fin.at[kind, rows]
            dst = dq_out.at[0, :, pl.ds(pl.multiple_of(head * 256 + kind * HEAD, HEAD), HEAD)]
        else:
            src, dst = dkv_fin.at[kind - 2, rows], (dk_out, dv_out)[kind - 2].at[0, :, wide(head, HEAD)]
        if r == 0:
            return pltpu.make_async_copy(src, dst, s_out.at[kind, 0])
        return remote(src, dst, s_out.at[kind, r], r_out.at[kind, r], (p, inner, outer))

    def finish_dq(e):
        for slot in (1, 2, 3):
            return_dq(slot, e).wait_recv()
        feats = slice(e * HEAD, (e + 1) * HEAD)
        for r in (4, 5, 6, 7, 1, 2, 3, 0):
            rows = wide(peer(r), PART)
            total = DQ[0, feats, rows]
            for slot in range(3):
                total = total + dq_recv[slot, feats, rows].astype(F32)
            dq_fin[e, rows, :] = (total * SCALE).T.astype(BF16)
            give(e, r).start()

    finish_dq(0)
    return_core(1).wait_recv()
    return_far().wait_recv()
    for r in (4, 5, 6, 7, 1, 2, 3, 0):
        rows = wide(peer(r), PART)
        for j, scale in ((0, SCALE), (1, 1.0)):
            total = DKV[0, j, rows, :] + core_recv[0, j, rows, :] + far_recv[j, rows, :].astype(F32)
            dkv_fin[j, rows, :] = (total * scale).astype(BF16)
        give(2, r).start()
        give(3, r).start()
    finish_dq(1)

    for r in range(1, 8):
        for i in range(3):
            exchange(i, r).wait_send()
    for slot in (1, 2, 3):
        for part in range(2):
            for what in ("stats", 0, 1) if slot == 3 else ("stats", 0):
                send_q(slot, part, what).wait_send()
            send_k(slot, part).wait_send()
        for e in range(2):
            return_dq(slot, e).wait_send()
    for slot in (1, 3):
        return_core(slot).wait_send()
    return_far().wait_send()
    for kind in range(4):
        for r in range(8):
            give(kind, r).wait()


def per_device(queries, key_input, value_input, outputs, output_gradient, log_sum_exp, block_order):
    any_space = pl.BlockSpec(memory_space=pl.ANY)
    dma = pltpu.SemaphoreType.DMA
    return pl.pallas_call(
        kernel,
        out_shape=(
            jax.ShapeDtypeStruct((1, PART, 2048), BF16),
            jax.ShapeDtypeStruct((1, PART, 1024), BF16),
            jax.ShapeDtypeStruct((1, PART, 1024), BF16),
        ),
        in_specs=[pl.BlockSpec(memory_space=pltpu.SMEM)]
        + [any_space] * 5
        + [pl.BlockSpec(memory_space=pltpu.VMEM)],
        out_specs=(any_space,) * 3,
        scratch_shapes=[
            pltpu.VMEM((PART, 2048), BF16),
            pltpu.VMEM((PART, 2048), BF16),
            pltpu.VMEM((HEADS, 2, PART, 256), BF16),
            pltpu.VMEM((HEADS, 2, PART, HEAD), BF16),
            pltpu.VMEM((HEADS, 8, PART), F32),
            pltpu.VMEM((4, 2, ROWS, 256), BF16),
            pltpu.VMEM((4, 2, ROWS, HEAD), BF16),
            pltpu.VMEM((4, 8, ROWS), F32),
            pltpu.VMEM((4, 256, ROWS), F32),
            pltpu.VMEM((4, 2, ROWS, HEAD), F32),
            pltpu.VMEM((3, 256, ROWS), BF16),
            pltpu.VMEM((3, 256, ROWS), BF16),
            pltpu.VMEM((2, 2, ROWS, HEAD), F32),
            pltpu.VMEM((2, ROWS, HEAD), BF16),
            pltpu.VMEM((2, ROWS, HEAD), BF16),
            pltpu.VMEM((2, ROWS, HEAD), BF16),
            pltpu.VMEM((2, ROWS, HEAD), BF16),
            dma((5, 8)),
            dma((3, 8)),
            dma((3, 8)),
            dma((4, 2, 3)),
            dma((4, 2, 3)),
            dma((4, 2)),
            dma((4, 2)),
            dma((4, 2)),
            dma((4, 2)),
            dma((4,)),
            dma((4,)),
            dma((4, 8)),
            dma((4, 8)),
        ],
        compiler_params=pltpu.CompilerParams(
            collective_id=0, has_side_effects=True, vmem_limit_bytes=56 * 1024 * 1024
        ),
        name="attention_backward",
    )(block_order, queries, key_input, value_input, outputs, output_gradient, jnp.transpose(log_sum_exp, (0, 2, 1)))


def solution(mesh):
    split = P(("inner", "outer"), "head", None)
    return jax.shard_map(
        per_device, mesh=mesh, in_specs=(split,) * 6 + (P(),), out_specs=(split,) * 3, check_vma=False
    )
```

```python
import functools

import jax
import jax.numpy as jnp
from jax import lax
from jax.experimental import pallas as pl
from jax.experimental.pallas import tpu as pltpu
from jax.sharding import PartitionSpec as P

MESH = pl.DeviceIdType.MESH
F32, BF16 = jnp.float32, jnp.bfloat16
HEAD = 128
HEADS = 8
PART = 128
HALF = 512
ROWS = 1024
LOG2E = 1.4426950408889634
SCALE = HEAD**-0.5
TILE = 256
NT = (((1,), (1,)), ((), ()))


def remote(src, dst, send_sem, recv_sem, device):
    return pltpu.make_async_remote_copy(
        src_ref=src,
        dst_ref=dst,
        send_sem=send_sem,
        recv_sem=recv_sem,
        device_id=device,
        device_id_type=MESH,
    )


def dot(a, b):
    return jnp.dot(a, b, preferred_element_type=F32)


def dot_nt(a, b):
    return lax.dot_general(a, b, NT, preferred_element_type=F32)


def block(q, do, stats, k, v, mask, heads):
    tiles = [(e, t) for e in heads for t in range(HALF // TILE)]

    def products(e, t):
        rows, feats = slice(t * TILE, (t + 1) * TILE), slice(e * HEAD, (e + 1) * HEAD)
        return dot_nt(k, q[rows, feats]), dot_nt(v, do[rows, feats])

    probs_low, score_grads = [], []
    ahead = products(*tiles[0])
    for n, (e, t) in enumerate(tiles):
        scores, prob_grad = ahead
        if n + 1 < len(tiles):
            ahead = products(*tiles[n + 1])
        cols = slice(t * TILE, (t + 1) * TILE)
        probs = jnp.exp2(scores * (SCALE * LOG2E) - stats[e : e + 1, cols])
        if mask:
            key_id = lax.broadcasted_iota(jnp.int32, (HALF, TILE), 0)
            query_id = lax.broadcasted_iota(jnp.int32, (HALF, TILE), 1) + t * TILE
            probs = jnp.where(key_id <= query_id, probs, 0.0)
        score_grads.append((probs * (prob_grad - stats[2 + e : 3 + e, cols])).astype(BF16))
        probs_low.append(probs.astype(BF16))
    probs_low = jnp.concatenate(probs_low, axis=1)
    score_grads = jnp.concatenate(score_grads, axis=1)

    def stacked(x):
        return jnp.concatenate([x[:, e * HEAD : (e + 1) * HEAD] for e in heads], axis=0)

    dv = dot(probs_low, stacked(do))
    dk = dot(score_grads, stacked(q))
    dq = dot(k.T, score_grads)
    return [(e, dq[:, i * HALF : (i + 1) * HALF]) for i, e in enumerate(heads)], dk, dv


def kernel(
    order,
    q_in,
    k_in,
    v_in,
    o_in,
    do_in,
    lse_in,
    dq_out,
    dk_out,
    dv_out,
    o_vm,
    do_vm,
    qd_send,
    kv_send,
    stat_send,
    far_stage,
    QD,
    KV,
    ST,
    DQ,
    DKV,
    dkv_send,
    dkv_recv,
    core_recv,
    dq_fin,
    dq_part,
    dkv_fin,
    s_loc,
    s_a2a,
    r_a2a,
    s_q,
    r_q,
    s_k,
    r_k,
    s_dq,
    r_dq,
    s_dk,
    r_dk,
    s_far,
    r_far,
    s_stage,
    r_stage,
    s_dqo,
    r_dqo,
    s_out,
    r_out,
):
    head, inner, outer = lax.axis_index("head"), lax.axis_index("inner"), lax.axis_index("outer")
    x_lo, z = head // 4, head % 4
    x_hi, core = outer // 2, outer % 2

    def peer(r):
        return ((x_lo + r // 4) % 2) * 4 + (z + r % 4) % 4

    k_dev = {
        1: (head, (inner + 1) % 4, outer),
        2: (head, (inner + 3) % 4, outer),
        3: (head, (inner + 2) % 4, outer),
    }
    back_dev = {1: k_dev[2], 2: k_dev[1], 3: k_dev[3]}
    core_dev = (head, inner, x_hi * 2 + (core + 1) % 2)
    far_outer = ((x_hi + 1) % 2) * 2 + core

    barrier = pltpu.get_barrier_semaphore()
    everyone = [(peer(r), inner, outer) for r in range(1, 8)] + [(peer(r), inner, far_outer) for r in range(8)]
    everyone += [k_dev[1], k_dev[2], k_dev[3], core_dev]
    for device in everyone:
        pl.semaphore_signal(barrier, inc=1, device_id=device, device_id_type=MESH)

    mine = pl.ds(pl.multiple_of(head * PART, PART), PART)

    def wide(p, n):
        return pl.ds(pl.multiple_of(p * n, n), n)

    def fetch(r, i):
        p = peer(r)
        src = (q_in, do_in, k_in, v_in)[i].at[0, :, wide(p, (256, 256, 128, 128)[i])]
        if r == 0:
            dst = (QD if i < 2 else KV).at[0, i % 2, mine]
        else:
            dst = (qd_send if i < 2 else kv_send).at[r, i % 2]
        return pltpu.make_async_copy(src, dst, s_loc.at[i, r])

    def exchange(i, r):
        p = peer(r)
        src, dst = [
            (qd_send.at[r], QD.at[0, :, mine]),
            (kv_send.at[r], KV.at[0, :, mine]),
            (stat_send.at[p], ST.at[0, :, mine]),
        ][i]
        return remote(src, dst, s_a2a.at[i, r], r_a2a.at[i, r], (p, inner, outer))

    def to_far(kind, r):
        p = peer(r)
        if kind == 0:
            src, dst = QD.at[0, :, mine] if r == 0 else qd_send.at[r], QD.at[2, :, mine]
        else:
            src, dst = stat_send.at[p], ST.at[2, :, mine]
        return remote(src, dst, s_far.at[kind, r], r_far.at[kind, r], (p, inner, far_outer))

    def to_stage():
        src = qd_send.at[pl.ds(5, 3)]
        return remote(src, far_stage, s_far.at[0, 5], r_far.at[0, 5], (peer(4), inner, far_outer))

    def from_stage(b):
        rows = wide(peer(4), PART)
        device = (x_lo * 4 + (z + b) % 4, inner, outer)
        return remote(far_stage.at[b - 1], QD.at[2, :, rows], s_stage.at[b], r_stage.at[b], device)

    turn = (4, 1, 5, 3, 7, 2, 6)
    for pick in ((2, 3), (0, 1)):
        for r in turn:
            for i in pick:
                fetch(r, i).start()
    for i in range(4):
        fetch(0, i).start()
    rows_in = [
        pltpu.make_async_copy(o_in.at[0], o_vm, s_loc.at[4, 0]),
        pltpu.make_async_copy(do_in.at[0], do_vm, s_loc.at[4, 1]),
    ]
    for copy in rows_in:
        copy.start()
    pl.semaphore_wait(barrier, len(everyone))
    for r in turn:
        for i in (2, 3):
            fetch(r, i).wait()
        exchange(1, r).start()

    for r in (4, 5, 6, 7):
        for i in (0, 1):
            fetch(r, i).wait()
    to_far(0, 4).start()
    to_stage().start()

    for copy in rows_in:
        copy.wait()
    lane = lax.broadcasted_iota(jnp.int32, (PART, 128), 1)
    delta = jnp.zeros((PART, 128), F32)
    for h in range(2 * HEADS):
        cols = slice(h * HEAD, (h + 1) * HEAD)
        total = jnp.sum(o_vm[:, cols].astype(F32) * do_vm[:, cols].astype(F32), axis=1, keepdims=True)
        delta = jnp.where(lane == h, total, delta)
    delta_t = delta.T
    lse_t = lse_in[0] * LOG2E
    stat_send[...] = jnp.zeros(stat_send.shape, F32)
    for g in range(HEADS):
        stat_send[g, 0:2, :] = lse_t[2 * g : 2 * g + 2, :]
        stat_send[g, 2:4, :] = delta_t[2 * g : 2 * g + 2, :]
    own_stat = pltpu.make_async_copy(stat_send.at[head], ST.at[0, :, mine], s_loc.at[4, 2])
    own_stat.start()
    for r in range(1, 8):
        exchange(2, r).start()
    for r in range(8):
        to_far(1, r).start()

    def clear(i, _):
        for s in range(4):
            DQ[s, pl.ds(pl.multiple_of(i * 32, 32), 32), :] = jnp.zeros((32, ROWS), F32)
            for j in range(2):
                DKV[s, j, pl.ds(pl.multiple_of(i * 128, 128), 128), :] = jnp.zeros((128, HEAD), F32)
        return 0

    lax.fori_loop(0, 8, clear, 0)

    LO, HI = 0, 1

    def half(part):
        return pl.ds(part * HALF, HALF)

    def send_q(slot, part, what):
        rows = half(part)
        array = ST if what else QD
        src = array.at[2 if slot == 3 else 0, :, rows]
        return remote(src, array.at[slot, :, rows], s_q.at[slot, part, what], r_q.at[slot, part, what], core_dev)

    def send_k(slot, part, what):
        rows = half(part)
        if slot < 3:
            src, dst = KV.at[0, :, rows], KV.at[slot, :, rows]
            return remote(src, dst, s_k.at[slot, part, 0], r_k.at[slot, part, 0], k_dev[slot])
        src, dst = KV.at[2 - what, what, rows], KV.at[3, what, rows]
        return remote(src, dst, s_k.at[3, part, what], r_k.at[3, part, what], k_dev[2 - what])

    def add_block(qs, q_lo, ks, k_lo, mask, heads=(0, 1)):
        q_rows, k_rows = pl.ds(q_lo, HALF), pl.ds(k_lo, HALF)
        dq, dk, dv = block(
            QD[qs, 0, q_rows, :],
            QD[qs, 1, q_rows, :],
            ST[qs, :, q_rows],
            KV[ks, 0, k_rows, :],
            KV[ks, 1, k_rows, :],
            mask,
            heads,
        )
        for e, part in dq:
            DQ[qs, e * HEAD : (e + 1) * HEAD, q_rows] += part
        DKV[ks, 0, k_rows, :] += dk
        DKV[ks, 1, k_rows, :] += dv

    def add_either(qs, ks, heads=(0, 1)):
        q_outer = ((x_hi + qs // 2) % 2) * 2 + (core + qs % 2) % 2
        k_inner = (inner + (ks + 1) // 2 + 2 * ((ks % 2) * (1 - ks // 2))) % 4
        sel = order[2 * (k_inner * 4 + outer)] < order[2 * (inner * 4 + q_outer)]

        def pick(lo, hi):
            return jnp.where(sel, lo, hi)

        dq, dk, dv = block(
            pick(QD[qs, 0, 0:HALF, :], QD[qs, 0, HALF:ROWS, :]),
            pick(QD[qs, 1, 0:HALF, :], QD[qs, 1, HALF:ROWS, :]),
            pick(ST[qs, :, 0:HALF], ST[qs, :, HALF:ROWS]),
            pick(KV[ks, 0, 0:HALF, :], KV[ks, 0, HALF:ROWS, :]),
            pick(KV[ks, 1, 0:HALF, :], KV[ks, 1, HALF:ROWS, :]),
            False,
            heads,
        )
        for e, part in dq:
            zero = jnp.zeros_like(part)
            rows = slice(e * HEAD, (e + 1) * HEAD)
            DQ[qs, rows, 0:HALF] += jnp.where(sel, part, zero)
            DQ[qs, rows, HALF:ROWS] += jnp.where(sel, zero, part)
        for j, part in enumerate((dk, dv)):
            zero = jnp.zeros_like(part)
            DKV[ks, j, 0:HALF, :] += jnp.where(sel, part, zero)
            DKV[ks, j, HALF:ROWS, :] += jnp.where(sel, zero, part)

    def add_full(qs, ks, heads=(0, 1)):
        add_block(qs, HALF, ks, 0, False, heads)

    def wait_half(part, kinds):
        base = 4 * ((1 - x_lo) if part == HI else x_lo)
        for j in range(4):

            def arrived(r=base + j):
                for kind in kinds:
                    exchange(kind, r).wait_recv()

            if j == 0:
                pl.when(base > 0)(arrived)
            else:
                arrived()

    def near_keys(part):
        for slot in (1, 2):
            send_k(slot, part, 0).wait_recv()
            send_k(3, part, 2 - slot).start()

    for r in turn:
        for i in (0, 1):
            if r < 4:
                fetch(r, i).wait()
        exchange(1, r).wait_send()
        exchange(0, r).start()
    for i in range(4):
        fetch(0, i).wait()
    for part in (LO, HI):
        wait_half(part, (1,))
        for slot in (1, 2):
            send_k(slot, part, 0).start()
    near_keys(LO)
    own_stat.wait()
    for part in (HI, LO):
        wait_half(part, (2, 0))
        for what in (1, 0):
            send_q(1, part, what).start()
    to_stage().wait_recv()
    for b in (1, 3, 2):
        from_stage(b).start()
        to_far(0, b).start()
    to_far(0, 0).start()

    def arrived_queries(slot, part):
        for what in (1, 0):
            send_q(slot, part, what).wait_recv()

    def far_to_core(part):
        crossed = (1 - x_lo) if part == HI else x_lo

        @pl.when(crossed == 1)
        def _():
            to_far_in(0, 4).wait_recv()
            for b in (1, 2, 3):
                from_stage(b).wait_recv()

        @pl.when(crossed == 0)
        def _():
            for r in range(4):
                to_far_in(0, r).wait_recv()

        for j in range(4):
            to_far_in(1, 4 * crossed + j).wait_recv()
        for what in (1, 0):
            send_q(3, part, what).start()

    def to_far_in(kind, r):
        dst = (ST if kind else QD).at[2, :, mine]
        return remote(dst, dst, s_far.at[kind, r], r_far.at[kind, r], (head, inner, far_outer))

    def return_core(slot, e):
        feats = pl.ds(e * HEAD, HEAD)
        src, dst = DQ.at[slot, feats], core_recv.at[slot // 2, feats]
        return remote(src, dst, s_dq.at[slot, e], r_dq.at[slot, e], core_dev)

    def return_dkv(slot, j):
        src, dst = dkv_send.at[slot - 1, j], dkv_recv.at[slot - 1, j]
        return remote(src, dst, s_dk.at[slot, j], r_dk.at[slot, j], back_dev[slot])

    def own_diagonal(i, _):
        at = pl.multiple_of(i * HALF, HALF)
        add_block(0, at, 0, at, True)
        return 0

    lax.fori_loop(0, 2, own_diagonal, 0)
    add_full(0, 0)
    near_keys(HI)
    for part in (HI, LO):
        arrived_queries(1, part)
    add_full(1, 0)
    add_either(1, 0)

    def near_queries(n, _):
        qs, ks = n % 2, 1 + n // 2

        for at, part in ((4, HI), (5, LO)):

            @pl.when(n == at)
            def _():
                far_to_core(part)

        @pl.when(n == 4)
        def _():
            for part in (LO, HI):
                for what in range(2):
                    send_k(3, part, what).wait_recv()

        add_full(qs, ks)
        add_either(qs, ks)
        return 0

    lax.fori_loop(0, 6, near_queries, 0)

    for e in range(2):
        return_core(1, e).start()
    back = (4, 1, 5, 3, 7, 2, 6, 0)

    def transpose_dq(far, e, r):
        rows, feats = wide(peer(r), PART), slice(e * HEAD, (e + 1) * HEAD)
        total = DQ[2 * far, feats, rows] + core_recv[far, feats, rows]
        dq_fin[far, e, rows, :] = (total * SCALE).T.astype(BF16)

    def give_dq(far, e, r):
        p = peer(r)
        src, dst = dq_fin.at[far, e, wide(p, PART)], dq_part.at[far, head, e]
        if not far and r == 0:
            return pltpu.make_async_copy(src, dst, s_dqo.at[0, e, 0])
        device = (p, inner, far_outer if far else outer)
        return remote(src, dst, s_dqo.at[far, e, r], r_dqo.at[far, e, r], device)

    def send_rows(far, e):
        return_core(3 if far else 1, e).wait_recv()
        for r in back:
            transpose_dq(far, e, r)
            give_dq(far, e, r).start()

    def far_queries(m, _):
        i = m // 2
        qs, ks = 2 + m % 2, i + 3 * ((3 - i) // 3)

        @pl.when(m == 1)
        def _():
            for part in (HI, LO):
                arrived_queries(3, part)

        add_full(qs, ks)
        add_either(qs, ks)
        @pl.when(m == 1)
        def _():
            for e in range(2):
                send_rows(0, e)

        for at, slot in ((1, 3), (3, 1), (5, 2)):

            @pl.when(m == at)
            def _():
                for j in range(2):

                    def step(i, _):
                        rows = pl.ds(pl.multiple_of(i * 128, 128), 128)
                        dkv_send[slot - 1, j, rows, :] = DKV[slot, j, rows, :].astype(BF16)
                        return 0

                    lax.fori_loop(0, 8, step, 0)
                    return_dkv(slot, j).start()

        return 0

    lax.fori_loop(0, 6, far_queries, 0)

    for e in range(2):
        add_full(3, 0, (e,))
        add_either(3, 0, (e,))
        return_core(3, e).start()
        if e == 1:
            send_rows(1, 0)
        add_full(2, 0, (e,))
        add_either(2, 0, (e,))
    send_rows(1, 1)

    def give(kind, r):
        p = peer(r)
        src, dst = dkv_fin.at[kind, wide(p, PART)], (dk_out, dv_out)[kind].at[0, :, wide(head, HEAD)]
        if r == 0:
            return pltpu.make_async_copy(src, dst, s_out.at[kind, 0])
        return remote(src, dst, s_out.at[kind, r], r_out.at[kind, r], (p, inner, outer))

    for j, scale in ((0, SCALE), (1, 1.0)):
        for slot in (3, 1, 2):
            return_dkv(slot, j).wait_recv()
        for r in back:
            rows = wide(peer(r), PART)
            total = DKV[0, j, rows, :]
            for slot in range(3):
                total = total + dkv_recv[slot, j, rows, :].astype(F32)
            dkv_fin[j, rows, :] = (total * scale).astype(BF16)
            give(j, r).start()

    for e in range(2):
        for far in range(2):
            for r in range(8):
                give_dq(far, e, r).wait()
        for g in range(HEADS):
            total = dq_part[0, g, e].astype(F32) + dq_part[1, g, e].astype(F32)
            dq_out[0, :, g * 256 + e * HEAD : g * 256 + (e + 1) * HEAD] = total.astype(BF16)

    for r in range(1, 8):
        for i in (0, 2):
            exchange(i, r).wait_send()
    for r in range(8):
        to_far(1, r).wait_send()
    for r in range(5):
        to_far(0, r).wait_send()
    to_stage().wait_send()
    for b in (1, 2, 3):
        from_stage(b).wait_send()
    for slot in (1, 2, 3):
        for part in range(2):
            for what in range(2):
                if slot != 2:
                    send_q(slot, part, what).wait_send()
            for what in range(2 if slot == 3 else 1):
                send_k(slot, part, what).wait_send()
        for j in range(2):
            return_dkv(slot, j).wait_send()
    for slot in (1, 3):
        for e in range(2):
            return_core(slot, e).wait_send()
    for kind in range(2):
        for r in range(8):
            give(kind, r).wait()


def copy_kernel(dq, dk, dv, dq_out, dk_out, dv_out):
    for src, dst in ((dq, dq_out), (dk, dk_out), (dv, dv_out)):
        dst[...] = src[...]


def per_device(queries, key_input, value_input, outputs, output_gradient, log_sum_exp, block_order):
    any_space = pl.BlockSpec(memory_space=pl.ANY)
    dma = pltpu.SemaphoreType.DMA
    grads = pl.pallas_call(
        kernel,
        out_shape=(
            jax.ShapeDtypeStruct((1, PART, 2048), BF16),
            jax.ShapeDtypeStruct((1, PART, 1024), BF16),
            jax.ShapeDtypeStruct((1, PART, 1024), BF16),
        ),
        in_specs=[pl.BlockSpec(memory_space=pltpu.SMEM)]
        + [any_space] * 5
        + [pl.BlockSpec(memory_space=pltpu.VMEM)],
        out_specs=(pl.BlockSpec(memory_space=pltpu.VMEM), any_space, any_space),
        scratch_shapes=[
            pltpu.VMEM((PART, 2048), BF16),
            pltpu.VMEM((PART, 2048), BF16),
            pltpu.VMEM((HEADS, 2, PART, 256), BF16),
            pltpu.VMEM((HEADS, 2, PART, HEAD), BF16),
            pltpu.VMEM((HEADS, 8, PART), F32),
            pltpu.VMEM((3, 2, PART, 256), BF16),
            pltpu.VMEM((4, 2, ROWS, 256), BF16),
            pltpu.VMEM((4, 2, ROWS, HEAD), BF16),
            pltpu.VMEM((4, 8, ROWS), F32),
            pltpu.VMEM((4, 256, ROWS), F32),
            pltpu.VMEM((4, 2, ROWS, HEAD), F32),
            pltpu.VMEM((3, 2, ROWS, HEAD), BF16),
            pltpu.VMEM((3, 2, ROWS, HEAD), BF16),
            pltpu.VMEM((2, 256, ROWS), F32),
            pltpu.VMEM((2, 2, ROWS, HEAD), BF16),
            pltpu.VMEM((2, HEADS, 2, PART, HEAD), BF16),
            pltpu.VMEM((2, ROWS, HEAD), BF16),
            dma((5, 8)),
            dma((3, 8)),
            dma((3, 8)),
            dma((4, 2, 2)),
            dma((4, 2, 2)),
            dma((4, 2, 2)),
            dma((4, 2, 2)),
            dma((4, 2)),
            dma((4, 2)),
            dma((4, 2)),
            dma((4, 2)),
            dma((2, 8)),
            dma((2, 8)),
            dma((4,)),
            dma((4,)),
            dma((2, 2, 8)),
            dma((2, 2, 8)),
            dma((2, 8)),
            dma((2, 8)),
        ],
        compiler_params=pltpu.CompilerParams(
            collective_id=0, has_side_effects=True, vmem_limit_bytes=56 * 1024 * 1024
        ),
        name="attention_backward",
    )(block_order, queries, key_input, value_input, outputs, output_gradient, jnp.transpose(log_sum_exp, (0, 2, 1)))
    whole = pl.BlockSpec(memory_space=pltpu.VMEM)
    return pl.pallas_call(
        copy_kernel,
        out_shape=tuple(jax.ShapeDtypeStruct(g.shape, g.dtype) for g in grads),
        in_specs=[whole] * 3,
        out_specs=(whole,) * 3,
        name="copy_out",
    )(*grads)


def solution(mesh):
    split = P(("inner", "outer"), "head", None)
    return jax.shard_map(
        per_device, mesh=mesh, in_specs=(split,) * 6 + (P(),), out_specs=(split,) * 3, check_vma=False
    )
```

```python
import functools

import jax
import jax.numpy as jnp
from jax import lax
from jax.experimental import pallas as pl
from jax.experimental.pallas import tpu as pltpu
from jax.sharding import PartitionSpec as P

MESH = pl.DeviceIdType.MESH
F32, BF16 = jnp.float32, jnp.bfloat16
HEAD = 128
HEADS = 8
PART = 128
HALF = 512
ROWS = 1024
LOG2E = 1.4426950408889634
SCALE = HEAD**-0.5
TILE = 256
NT = (((1,), (1,)), ((), ()))


def remote(src, dst, send_sem, recv_sem, device):
    return pltpu.make_async_remote_copy(
        src_ref=src,
        dst_ref=dst,
        send_sem=send_sem,
        recv_sem=recv_sem,
        device_id=device,
        device_id_type=MESH,
    )


def dot(a, b):
    return jnp.dot(a, b, preferred_element_type=F32)


def dot_nt(a, b):
    return lax.dot_general(a, b, NT, preferred_element_type=F32)


def block(q, do, stats, k, v, mask, heads):
    queries, keys = q.shape[0], k.shape[0]
    tiles = [(e, t) for e in heads for t in range(queries // TILE)]

    def products(e, t):
        rows, feats = slice(t * TILE, (t + 1) * TILE), slice(e * HEAD, (e + 1) * HEAD)
        return dot_nt(k, q[rows, feats]), dot_nt(v, do[rows, feats])

    probs_low, score_grads = [], []
    ahead = products(*tiles[0])
    for n, (e, t) in enumerate(tiles):
        scores, prob_grad = ahead
        if n + 1 < len(tiles):
            ahead = products(*tiles[n + 1])
        cols = slice(t * TILE, (t + 1) * TILE)
        probs = jnp.exp2(scores * (SCALE * LOG2E) - stats[e : e + 1, cols])
        if mask and t * TILE < keys:
            key_id = lax.broadcasted_iota(jnp.int32, (keys, TILE), 0)
            query_id = lax.broadcasted_iota(jnp.int32, (keys, TILE), 1) + t * TILE
            probs = jnp.where(key_id <= query_id, probs, 0.0)
        score_grads.append((probs * (prob_grad - stats[2 + e : 3 + e, cols])).astype(BF16))
        probs_low.append(probs.astype(BF16))
    probs_low = jnp.concatenate(probs_low, axis=1)
    score_grads = jnp.concatenate(score_grads, axis=1)

    def stacked(x):
        return jnp.concatenate([x[:, e * HEAD : (e + 1) * HEAD] for e in heads], axis=0)

    dv = dot(probs_low, stacked(do))
    dk = dot(score_grads, stacked(q))
    dq = dot(k.T, score_grads)
    return [(e, dq[:, i * queries : (i + 1) * queries]) for i, e in enumerate(heads)], dk, dv


def kernel(
    order,
    q_in,
    k_in,
    v_in,
    o_in,
    do_in,
    lse_in,
    dq_out,
    dk_out,
    dv_out,
    o_vm,
    do_vm,
    qd_send,
    kv_send,
    stat_send,
    far_stage,
    QD,
    KV,
    ST,
    DQ,
    DKV,
    dkv_send,
    dkv_recv,
    core_recv,
    dq_fin,
    dq_part,
    dkv_fin,
    s_loc,
    s_a2a,
    r_a2a,
    s_q,
    r_q,
    s_k,
    r_k,
    s_dq,
    r_dq,
    s_dk,
    r_dk,
    s_far,
    r_far,
    s_stage,
    r_stage,
    s_dqo,
    r_dqo,
    s_out,
    r_out,
):
    head, inner, outer = lax.axis_index("head"), lax.axis_index("inner"), lax.axis_index("outer")
    x_lo, z = head // 4, head % 4
    x_hi, core = outer // 2, outer % 2

    def peer(r):
        return ((x_lo + r // 4) % 2) * 4 + (z + r % 4) % 4

    k_dev = {
        1: (head, (inner + 1) % 4, outer),
        2: (head, (inner + 3) % 4, outer),
        3: (head, (inner + 2) % 4, outer),
    }
    back_dev = {1: k_dev[2], 2: k_dev[1], 3: k_dev[3]}
    core_dev = (head, inner, x_hi * 2 + (core + 1) % 2)
    far_outer = ((x_hi + 1) % 2) * 2 + core

    barrier = pltpu.get_barrier_semaphore()
    everyone = [(peer(r), inner, outer) for r in range(1, 8)] + [(peer(r), inner, far_outer) for r in range(8)]
    everyone += [k_dev[1], k_dev[2], k_dev[3], core_dev]
    for device in everyone:
        pl.semaphore_signal(barrier, inc=1, device_id=device, device_id_type=MESH)

    mine = pl.ds(pl.multiple_of(head * PART, PART), PART)

    def wide(p, n):
        return pl.ds(pl.multiple_of(p * n, n), n)

    def fetch(r, i):
        p = peer(r)
        src = (q_in, do_in, k_in, v_in)[i].at[0, :, wide(p, (256, 256, 128, 128)[i])]
        if r == 0:
            dst = (QD if i < 2 else KV).at[0, i % 2, mine]
        else:
            dst = (qd_send if i < 2 else kv_send).at[r, i % 2]
        return pltpu.make_async_copy(src, dst, s_loc.at[i, r])

    def exchange(i, r):
        p = peer(r)
        src, dst = [
            (qd_send.at[r], QD.at[0, :, mine]),
            (kv_send.at[r], KV.at[0, :, mine]),
            (stat_send.at[p], ST.at[0, :, mine]),
        ][i]
        return remote(src, dst, s_a2a.at[i, r], r_a2a.at[i, r], (p, inner, outer))

    def to_far(kind, r):
        p = peer(r)
        if kind == 0:
            src, dst = QD.at[0, :, mine] if r == 0 else qd_send.at[r], QD.at[2, :, mine]
        else:
            src, dst = stat_send.at[p], ST.at[2, :, mine]
        return remote(src, dst, s_far.at[kind, r], r_far.at[kind, r], (p, inner, far_outer))

    def to_stage():
        src = qd_send.at[pl.ds(5, 3)]
        return remote(src, far_stage, s_far.at[0, 5], r_far.at[0, 5], (peer(4), inner, far_outer))

    def from_stage(b):
        rows = wide(peer(4), PART)
        device = (x_lo * 4 + (z + b) % 4, inner, outer)
        return remote(far_stage.at[b - 1], QD.at[2, :, rows], s_stage.at[b], r_stage.at[b], device)

    turn = (4, 1, 5, 3, 7, 2, 6)
    for pick in ((2, 3), (0, 1)):
        for r in turn:
            for i in pick:
                fetch(r, i).start()
    for i in range(4):
        fetch(0, i).start()
    rows_in = [
        pltpu.make_async_copy(o_in.at[0], o_vm, s_loc.at[4, 0]),
        pltpu.make_async_copy(do_in.at[0], do_vm, s_loc.at[4, 1]),
    ]
    for copy in rows_in:
        copy.start()
    pl.semaphore_wait(barrier, len(everyone))
    for r in turn:
        for i in (2, 3):
            fetch(r, i).wait()
        exchange(1, r).start()

    for r in (4, 5, 6, 7):
        for i in (0, 1):
            fetch(r, i).wait()
    to_far(0, 4).start()
    to_stage().start()

    for copy in rows_in:
        copy.wait()
    lane = lax.broadcasted_iota(jnp.int32, (PART, 128), 1)
    delta = jnp.zeros((PART, 128), F32)
    for h in range(2 * HEADS):
        cols = slice(h * HEAD, (h + 1) * HEAD)
        total = jnp.sum(o_vm[:, cols].astype(F32) * do_vm[:, cols].astype(F32), axis=1, keepdims=True)
        delta = jnp.where(lane == h, total, delta)
    delta_t = delta.T
    lse_t = lse_in[0] * LOG2E
    stat_send[...] = jnp.zeros(stat_send.shape, F32)
    for g in range(HEADS):
        stat_send[g, 0:2, :] = lse_t[2 * g : 2 * g + 2, :]
        stat_send[g, 2:4, :] = delta_t[2 * g : 2 * g + 2, :]
    own_stat = pltpu.make_async_copy(stat_send.at[head], ST.at[0, :, mine], s_loc.at[4, 2])
    own_stat.start()
    for r in range(1, 8):
        exchange(2, r).start()
    for r in range(8):
        to_far(1, r).start()

    def clear(i, _):
        for s in range(4):
            DQ[s, pl.ds(pl.multiple_of(i * 32, 32), 32), :] = jnp.zeros((32, ROWS), F32)
            for j in range(2):
                DKV[s, j, pl.ds(pl.multiple_of(i * 128, 128), 128), :] = jnp.zeros((128, HEAD), F32)
        return 0


    LO, HI = 0, 1

    def half(part):
        return pl.ds(pl.multiple_of(part * HALF, HALF), HALF)

    def send_q(slot, part, what):
        rows = half(part)
        array = ST if what else QD
        src = array.at[2 if slot == 3 else 0, :, rows]
        return remote(src, array.at[slot, :, rows], s_q.at[slot, part, what], r_q.at[slot, part, what], core_dev)

    def send_k(slot, part, what):
        rows = half(part)
        if slot < 3:
            src, dst = KV.at[0, :, rows], KV.at[slot, :, rows]
            return remote(src, dst, s_k.at[slot, part, 0], r_k.at[slot, part, 0], k_dev[slot])
        src, dst = KV.at[2 - what, what, rows], KV.at[3, what, rows]
        return remote(src, dst, s_k.at[3, part, what], r_k.at[3, part, what], k_dev[2 - what])

    def add_block(qs, q_lo, ks, k_lo, mask, queries=HALF, keys=HALF):
        q_rows, k_rows = pl.ds(q_lo, queries), pl.ds(k_lo, keys)
        dq, dk, dv = block(
            QD[qs, 0, q_rows, :],
            QD[qs, 1, q_rows, :],
            ST[qs, :, q_rows],
            KV[ks, 0, k_rows, :],
            KV[ks, 1, k_rows, :],
            mask,
            (0, 1),
        )
        for e, part in dq:
            DQ[qs, e * HEAD : (e + 1) * HEAD, q_rows] += part
        DKV[ks, 0, k_rows, :] += dk
        DKV[ks, 1, k_rows, :] += dv

    def visible_lower(qs, ks):
        q_outer = ((x_hi + qs // 2) % 2) * 2 + (core + qs % 2) % 2
        k_inner = (inner + (ks + 1) // 2 + 2 * ((ks % 2) * (1 - ks // 2))) % 4
        return order[2 * (k_inner * 4 + outer)] < order[2 * (inner * 4 + q_outer)]

    def add_pair(qs, ks, heads=(0, 1)):
        sel = visible_lower(qs, ks)

        def pick(lo, hi):
            return jnp.where(sel, lo, hi)

        q, do, stats = QD[qs, 0], QD[qs, 1], ST[qs]
        k, v = KV[ks, 0], KV[ks, 1]
        dq, dk, dv = block(q[HALF:], do[HALF:], stats[:, HALF:], k[:HALF], v[:HALF], False, heads)
        dq2, dk2, dv2 = block(
            pick(q[:HALF], q[HALF:]),
            pick(do[:HALF], do[HALF:]),
            pick(stats[:, :HALF], stats[:, HALF:]),
            pick(k[:HALF], k[HALF:]),
            pick(v[:HALF], v[HALF:]),
            False,
            heads,
        )
        for (e, upper), (_, part) in zip(dq, dq2):
            zero = jnp.zeros_like(part)
            rows = slice(e * HEAD, (e + 1) * HEAD)
            DQ[qs, rows, 0:HALF] += jnp.where(sel, part, zero)
            DQ[qs, rows, HALF:ROWS] += upper + jnp.where(sel, zero, part)
        for j, (lower, part) in enumerate(((dk, dk2), (dv, dv2))):
            zero = jnp.zeros_like(part)
            DKV[ks, j, 0:HALF, :] += lower + jnp.where(sel, part, zero)
            DKV[ks, j, HALF:ROWS, :] += jnp.where(sel, zero, part)

    def own_diagonal(which):
        at = pl.multiple_of(which * HALF, HALF)
        add_block(0, at, 0, at, True, HALF, TILE)
        at = pl.multiple_of(which * HALF + TILE, TILE)
        add_block(0, at, 0, at, True, TILE, TILE)

    def wait_half(part, kinds):
        base = 4 * ((1 - x_lo) if part == HI else x_lo)
        for j in range(4):

            def arrived(r=base + j):
                for kind in kinds:
                    exchange(kind, r).wait_recv()

            if j == 0:
                pl.when(base > 0)(arrived)
            else:
                arrived()

    def near_keys(part):
        for slot in (1, 2):
            send_k(slot, part, 0).wait_recv()
            send_k(3, part, 2 - slot).start()

    for r in turn:
        exchange(1, r).wait_send()
    for r in (1, 3, 2, 4, 5, 7, 6):
        for i in (0, 1):
            if r < 4:
                fetch(r, i).wait()
        exchange(0, r).start()
    lax.fori_loop(0, 8, clear, 0)
    for i in range(4):
        fetch(0, i).wait()
    for part in (LO, HI):
        wait_half(part, (1,))
        for slot in (1, 2):
            send_k(slot, part, 0).start()
    near_keys(LO)
    own_stat.wait()
    for part, group in ((x_lo, (1, 2, 3)), (1 - x_lo, (4, 5, 6, 7))):
        for r in group:
            for kind in (2, 0):
                exchange(kind, r).wait_recv()
        for what in (1, 0):
            send_q(1, part, what).start()
        if group[0] == 1:
            own_diagonal(x_lo)
    to_stage().wait_recv()
    for b in (1, 3, 2):
        from_stage(b).start()
        to_far(0, b).start()
    to_far(0, 0).start()

    def arrived_queries(slot, part):
        for what in (1, 0):
            send_q(slot, part, what).wait_recv()

    def far_to_core(part):
        crossed = (1 - x_lo) if part == HI else x_lo

        @pl.when(crossed == 1)
        def _():
            to_far_in(0, 4).wait_recv()
            for b in (1, 2, 3):
                from_stage(b).wait_recv()

        @pl.when(crossed == 0)
        def _():
            for r in range(4):
                to_far_in(0, r).wait_recv()

        for j in range(4):
            to_far_in(1, 4 * crossed + j).wait_recv()
        for what in (1, 0):
            send_q(3, part, what).start()

    def to_far_in(kind, r):
        dst = (ST if kind else QD).at[2, :, mine]
        return remote(dst, dst, s_far.at[kind, r], r_far.at[kind, r], (head, inner, far_outer))

    def return_core(slot, e):
        feats = pl.ds(e * HEAD, HEAD)
        src, dst = DQ.at[slot, feats], core_recv.at[slot // 2, feats]
        return remote(src, dst, s_dq.at[slot, e], r_dq.at[slot, e], core_dev)

    def return_dkv(slot, j):
        src, dst = dkv_send.at[slot - 1, j], dkv_recv.at[slot - 1, j]
        return remote(src, dst, s_dk.at[slot, j], r_dk.at[slot, j], back_dev[slot])

    own_diagonal(1 - x_lo)
    add_block(0, HALF, 0, 0, False)
    near_keys(HI)
    for part in (HI, LO):
        arrived_queries(1, part)
    add_pair(1, 0)

    def near_queries(n, _):
        qs, ks = n % 2, 1 + n // 2

        for at, part in ((4, HI), (5, LO)):

            @pl.when(n == at)
            def _():
                far_to_core(part)

        @pl.when(n == 4)
        def _():
            for part in (LO, HI):
                for what in range(2):
                    send_k(3, part, what).wait_recv()

        add_pair(qs, ks)
        return 0

    lax.fori_loop(0, 6, near_queries, 0)

    for e in range(2):
        return_core(1, e).start()
    back = (4, 1, 5, 3, 7, 2, 6, 0)

    def transpose_dq(far, e, r):
        rows, feats = wide(peer(r), PART), slice(e * HEAD, (e + 1) * HEAD)
        total = DQ[2 * far, feats, rows] + core_recv[far, feats, rows]
        dq_fin[far, e, rows, :] = (total * SCALE).T.astype(BF16)

    def give_dq(far, e, r):
        p = peer(r)
        src, dst = dq_fin.at[far, e, wide(p, PART)], dq_part.at[far, head, e]
        if not far and r == 0:
            return pltpu.make_async_copy(src, dst, s_dqo.at[0, e, 0])
        device = (p, inner, far_outer if far else outer)
        return remote(src, dst, s_dqo.at[far, e, r], r_dqo.at[far, e, r], device)

    def send_rows(far, e):
        return_core(3 if far else 1, e).wait_recv()
        for r in back:
            transpose_dq(far, e, r)
            give_dq(far, e, r).start()

    def far_queries(m, _):
        i = m // 2
        qs, ks = 2 + m % 2, i + 3 * ((3 - i) // 3)

        @pl.when(m == 1)
        def _():
            for part in (HI, LO):
                arrived_queries(3, part)

        add_pair(qs, ks)
        @pl.when(m == 1)
        def _():
            for e in range(2):
                send_rows(0, e)

        for at, slot in ((1, 3), (3, 1), (5, 2)):

            @pl.when(m == at)
            def _():
                for j in range(2):

                    def step(i, _):
                        rows = pl.ds(pl.multiple_of(i * 128, 128), 128)
                        dkv_send[slot - 1, j, rows, :] = DKV[slot, j, rows, :].astype(BF16)
                        return 0

                    lax.fori_loop(0, 8, step, 0)
                    return_dkv(slot, j).start()

        return 0

    lax.fori_loop(0, 6, far_queries, 0)

    for e in range(2):
        add_pair(3, 0, (e,))
        return_core(3, e).start()
        if e == 1:
            send_rows(1, 0)
        add_pair(2, 0, (e,))
    send_rows(1, 1)

    def give(kind, r):
        p = peer(r)
        src, dst = dkv_fin.at[kind, wide(p, PART)], (dk_out, dv_out)[kind].at[0, :, wide(head, HEAD)]
        if r == 0:
            return pltpu.make_async_copy(src, dst, s_out.at[kind, 0])
        return remote(src, dst, s_out.at[kind, r], r_out.at[kind, r], (p, inner, outer))

    for j, scale in ((0, SCALE), (1, 1.0)):
        for slot in (3, 1, 2):
            return_dkv(slot, j).wait_recv()
        for r in back:
            rows = wide(peer(r), PART)
            total = DKV[0, j, rows, :]
            for slot in range(3):
                total = total + dkv_recv[slot, j, rows, :].astype(F32)
            dkv_fin[j, rows, :] = (total * scale).astype(BF16)
            give(j, r).start()

    for e in range(2):
        for far in range(2):
            for r in range(8):
                give_dq(far, e, r).wait()
        for g in range(HEADS):
            total = dq_part[0, g, e].astype(F32) + dq_part[1, g, e].astype(F32)
            dq_out[0, :, g * 256 + e * HEAD : g * 256 + (e + 1) * HEAD] = total.astype(BF16)

    for r in range(1, 8):
        for i in (0, 2):
            exchange(i, r).wait_send()
    for r in range(8):
        to_far(1, r).wait_send()
    for r in range(5):
        to_far(0, r).wait_send()
    to_stage().wait_send()
    for b in (1, 2, 3):
        from_stage(b).wait_send()
    for slot in (1, 2, 3):
        for part in range(2):
            for what in range(2):
                if slot != 2:
                    send_q(slot, part, what).wait_send()
            for what in range(2 if slot == 3 else 1):
                send_k(slot, part, what).wait_send()
        for j in range(2):
            return_dkv(slot, j).wait_send()
    for slot in (1, 3):
        for e in range(2):
            return_core(slot, e).wait_send()
    for kind in range(2):
        for r in range(8):
            give(kind, r).wait()


def copy_kernel(dq, dk, dv, dq_out, dk_out, dv_out, dq_vm, dk_vm, dv_vm, sem):
    steps = []
    for i, (src, via, dst) in enumerate(((dq, dq_vm, dq_out), (dk, dk_vm, dk_out), (dv, dv_vm, dv_out))):
        for j in range(2):
            rows = pl.ds(j * PART // 2, PART // 2)
            n = 2 * i + j
            arrive = pltpu.make_async_copy(src.at[:, rows], via.at[:, rows], sem.at[0, n])
            leave = pltpu.make_async_copy(via.at[:, rows], dst.at[:, rows], sem.at[1, n])
            steps.append((arrive, leave))
    for arrive, _ in steps:
        arrive.start()
    for arrive, leave in steps:
        arrive.wait()
        leave.start()
    for _, leave in steps:
        leave.wait()


def per_device(queries, key_input, value_input, outputs, output_gradient, log_sum_exp, block_order):
    any_space = pl.BlockSpec(memory_space=pl.ANY)
    dma = pltpu.SemaphoreType.DMA
    grads = pl.pallas_call(
        kernel,
        out_shape=(
            jax.ShapeDtypeStruct((1, PART, 2048), BF16),
            jax.ShapeDtypeStruct((1, PART, 1024), BF16),
            jax.ShapeDtypeStruct((1, PART, 1024), BF16),
        ),
        in_specs=[pl.BlockSpec(memory_space=pltpu.SMEM)]
        + [any_space] * 5
        + [pl.BlockSpec(memory_space=pltpu.VMEM)],
        out_specs=(pl.BlockSpec(memory_space=pltpu.VMEM), any_space, any_space),
        scratch_shapes=[
            pltpu.VMEM((PART, 2048), BF16),
            pltpu.VMEM((PART, 2048), BF16),
            pltpu.VMEM((HEADS, 2, PART, 256), BF16),
            pltpu.VMEM((HEADS, 2, PART, HEAD), BF16),
            pltpu.VMEM((HEADS, 8, PART), F32),
            pltpu.VMEM((3, 2, PART, 256), BF16),
            pltpu.VMEM((4, 2, ROWS, 256), BF16),
            pltpu.VMEM((4, 2, ROWS, HEAD), BF16),
            pltpu.VMEM((4, 8, ROWS), F32),
            pltpu.VMEM((4, 256, ROWS), F32),
            pltpu.VMEM((4, 2, ROWS, HEAD), F32),
            pltpu.VMEM((3, 2, ROWS, HEAD), BF16),
            pltpu.VMEM((3, 2, ROWS, HEAD), BF16),
            pltpu.VMEM((2, 256, ROWS), F32),
            pltpu.VMEM((2, 2, ROWS, HEAD), BF16),
            pltpu.VMEM((2, HEADS, 2, PART, HEAD), BF16),
            pltpu.VMEM((2, ROWS, HEAD), BF16),
            dma((5, 8)),
            dma((3, 8)),
            dma((3, 8)),
            dma((4, 2, 2)),
            dma((4, 2, 2)),
            dma((4, 2, 2)),
            dma((4, 2, 2)),
            dma((4, 2)),
            dma((4, 2)),
            dma((4, 2)),
            dma((4, 2)),
            dma((2, 8)),
            dma((2, 8)),
            dma((4,)),
            dma((4,)),
            dma((2, 2, 8)),
            dma((2, 2, 8)),
            dma((2, 8)),
            dma((2, 8)),
        ],
        compiler_params=pltpu.CompilerParams(
            collective_id=0, has_side_effects=True, vmem_limit_bytes=56 * 1024 * 1024
        ),
        name="attention_backward",
    )(block_order, queries, key_input, value_input, outputs, output_gradient, jnp.transpose(log_sum_exp, (0, 2, 1)))
    return pl.pallas_call(
        copy_kernel,
        out_shape=tuple(jax.ShapeDtypeStruct(g.shape, g.dtype) for g in grads),
        in_specs=[any_space] * 3,
        out_specs=(any_space,) * 3,
        scratch_shapes=[pltpu.VMEM(g.shape, g.dtype) for g in grads] + [dma((2, 6))],
        name="copy_out",
    )(*grads)


def solution(mesh):
    split = P(("inner", "outer"), "head", None)
    return jax.shard_map(
        per_device, mesh=mesh, in_specs=(split,) * 6 + (P(),), out_specs=(split,) * 3, check_vma=False
    )
```

```python
import functools

import jax
import jax.numpy as jnp
from jax import lax
from jax.experimental import pallas as pl
from jax.experimental.pallas import tpu as pltpu
from jax.sharding import PartitionSpec as P

MESH = pl.DeviceIdType.MESH
F32, BF16 = jnp.float32, jnp.bfloat16
HEAD = 128
HEADS = 8
PART = 128
HALF = 512
ROWS = 1024
LOG2E = 1.4426950408889634
SCALE = HEAD**-0.5
TILE = 256
NT = (((1,), (1,)), ((), ()))


def remote(src, dst, send_sem, recv_sem, device):
    return pltpu.make_async_remote_copy(
        src_ref=src,
        dst_ref=dst,
        send_sem=send_sem,
        recv_sem=recv_sem,
        device_id=device,
        device_id_type=MESH,
    )


def dot(a, b):
    return jnp.dot(a, b, preferred_element_type=F32)


def dot_nt(a, b):
    return lax.dot_general(a, b, NT, preferred_element_type=F32)


def block(q, do, stats, k, v, mask, heads):
    queries, keys = q.shape[0], k.shape[0]
    tiles = [(e, t) for e in heads for t in range(queries // TILE)]

    def products(e, t):
        rows, feats = slice(t * TILE, (t + 1) * TILE), slice(e * HEAD, (e + 1) * HEAD)
        return dot_nt(k, q[rows, feats]), dot_nt(v, do[rows, feats])

    probs_low, score_grads = [], []
    ahead = products(*tiles[0])
    for n, (e, t) in enumerate(tiles):
        scores, prob_grad = ahead
        if n + 1 < len(tiles):
            ahead = products(*tiles[n + 1])
        cols = slice(t * TILE, (t + 1) * TILE)
        probs = jnp.exp2(scores * (SCALE * LOG2E) - stats[e : e + 1, cols])
        if mask and t * TILE < keys:
            key_id = lax.broadcasted_iota(jnp.int32, (keys, TILE), 0)
            query_id = lax.broadcasted_iota(jnp.int32, (keys, TILE), 1) + t * TILE
            probs = jnp.where(key_id <= query_id, probs, 0.0)
        score_grads.append((probs * (prob_grad - stats[2 + e : 3 + e, cols])).astype(BF16))
        probs_low.append(probs.astype(BF16))
    probs_low = jnp.concatenate(probs_low, axis=1)
    score_grads = jnp.concatenate(score_grads, axis=1)

    def stacked(x):
        return jnp.concatenate([x[:, e * HEAD : (e + 1) * HEAD] for e in heads], axis=0)

    dv = dot(probs_low, stacked(do))
    dk = dot(score_grads, stacked(q))
    dq = dot(k.T, score_grads)
    return [(e, dq[:, i * queries : (i + 1) * queries]) for i, e in enumerate(heads)], dk, dv


def kernel(
    order,
    q_in,
    k_in,
    v_in,
    o_in,
    do_in,
    lse_in,
    dq_out,
    dk_out,
    dv_out,
    o_vm,
    do_vm,
    qd_send,
    kv_send,
    stat_send,
    far_stage,
    QD,
    KV,
    ST,
    DQ,
    DKV,
    dkv_send,
    dkv_recv,
    core_recv,
    dq_fin,
    dq_part,
    dkv_fin,
    s_loc,
    s_a2a,
    r_a2a,
    s_q,
    r_q,
    s_k,
    r_k,
    s_dq,
    r_dq,
    s_dk,
    r_dk,
    s_far,
    r_far,
    s_stage,
    r_stage,
    s_dqo,
    r_dqo,
    s_out,
    r_out,
):
    head, inner, outer = lax.axis_index("head"), lax.axis_index("inner"), lax.axis_index("outer")
    x_lo, z = head // 4, head % 4
    x_hi, core = outer // 2, outer % 2

    def peer(r):
        return ((x_lo + r // 4) % 2) * 4 + (z + r % 4) % 4

    k_dev = {
        1: (head, (inner + 1) % 4, outer),
        2: (head, (inner + 3) % 4, outer),
        3: (head, (inner + 2) % 4, outer),
    }
    back_dev = {1: k_dev[2], 2: k_dev[1], 3: k_dev[3]}
    core_dev = (head, inner, x_hi * 2 + (core + 1) % 2)
    far_outer = ((x_hi + 1) % 2) * 2 + core

    barrier = pltpu.get_barrier_semaphore()
    everyone = [(peer(r), inner, outer) for r in range(1, 8)] + [(peer(r), inner, far_outer) for r in range(8)]
    everyone += [k_dev[1], k_dev[2], k_dev[3], core_dev]
    for device in everyone:
        pl.semaphore_signal(barrier, inc=1, device_id=device, device_id_type=MESH)

    mine = pl.ds(pl.multiple_of(head * PART, PART), PART)

    def wide(p, n):
        return pl.ds(pl.multiple_of(p * n, n), n)

    def fetch(r, i):
        p = peer(r)
        src = (q_in, do_in, k_in, v_in)[i].at[0, :, wide(p, (256, 256, 128, 128)[i])]
        if r == 0:
            dst = (QD if i < 2 else KV).at[0, i % 2, mine]
        else:
            dst = (qd_send if i < 2 else kv_send).at[r, i % 2]
        return pltpu.make_async_copy(src, dst, s_loc.at[i, r])

    def exchange(i, r):
        p = peer(r)
        src, dst = [
            (qd_send.at[r], QD.at[0, :, mine]),
            (kv_send.at[r], KV.at[0, :, mine]),
            (stat_send.at[p], ST.at[0, :, mine]),
        ][i]
        return remote(src, dst, s_a2a.at[i, r], r_a2a.at[i, r], (p, inner, outer))

    def to_far(kind, r):
        p = peer(r)
        if kind == 0:
            src, dst = QD.at[0, :, mine] if r == 0 else qd_send.at[r], QD.at[2, :, mine]
        else:
            src, dst = stat_send.at[p], ST.at[2, :, mine]
        return remote(src, dst, s_far.at[kind, r], r_far.at[kind, r], (p, inner, far_outer))

    def to_stage():
        src = qd_send.at[pl.ds(5, 3)]
        return remote(src, far_stage, s_far.at[0, 5], r_far.at[0, 5], (peer(4), inner, far_outer))

    def from_stage(b):
        rows = wide(peer(4), PART)
        device = (x_lo * 4 + (z + b) % 4, inner, outer)
        return remote(far_stage.at[b - 1], QD.at[2, :, rows], s_stage.at[b], r_stage.at[b], device)

    turn = (1, 3, 2, 4, 5, 7, 6)
    for pick in ((2, 3), (0, 1)):
        for r in turn:
            for i in pick:
                fetch(r, i).start()
    for i in range(4):
        fetch(0, i).start()
    rows_in = [
        pltpu.make_async_copy(o_in.at[0], o_vm, s_loc.at[4, 0]),
        pltpu.make_async_copy(do_in.at[0], do_vm, s_loc.at[4, 1]),
    ]
    for copy in rows_in:
        copy.start()
    pl.semaphore_wait(barrier, len(everyone))
    for r in turn:
        for i in (2, 3):
            fetch(r, i).wait()
        exchange(1, r).start()

    for r in (4, 5, 6, 7):
        for i in (0, 1):
            fetch(r, i).wait()
    to_far(0, 4).start()
    to_stage().start()

    for copy in rows_in:
        copy.wait()
    lane = lax.broadcasted_iota(jnp.int32, (PART, 128), 1)
    delta = jnp.zeros((PART, 128), F32)
    for h in range(2 * HEADS):
        cols = slice(h * HEAD, (h + 1) * HEAD)
        total = jnp.sum(o_vm[:, cols].astype(F32) * do_vm[:, cols].astype(F32), axis=1, keepdims=True)
        delta = jnp.where(lane == h, total, delta)
    delta_t = delta.T
    lse_t = lse_in[0] * LOG2E
    stat_send[...] = jnp.zeros(stat_send.shape, F32)
    for g in range(HEADS):
        stat_send[g, 0:2, :] = lse_t[2 * g : 2 * g + 2, :]
        stat_send[g, 2:4, :] = delta_t[2 * g : 2 * g + 2, :]
    own_stat = pltpu.make_async_copy(stat_send.at[head], ST.at[0, :, mine], s_loc.at[4, 2])
    own_stat.start()
    for r in range(1, 8):
        exchange(2, r).start()
    for r in range(8):
        to_far(1, r).start()

    def clear(i, _):
        for s in range(4):
            DQ[s, pl.ds(pl.multiple_of(i * 32, 32), 32), :] = jnp.zeros((32, ROWS), F32)
            for j in range(2):
                DKV[s, j, pl.ds(pl.multiple_of(i * 128, 128), 128), :] = jnp.zeros((128, HEAD), F32)
        return 0


    LO, HI = 0, 1

    def half(part):
        return pl.ds(pl.multiple_of(part * HALF, HALF), HALF)

    def send_q(slot, part, what):
        rows = half(part)
        array = ST if what else QD
        src = array.at[2 if slot == 3 else 0, :, rows]
        return remote(src, array.at[slot, :, rows], s_q.at[slot, part, what], r_q.at[slot, part, what], core_dev)

    def send_k(slot, part, what):
        rows = half(part)
        if slot < 3:
            src, dst = KV.at[0, :, rows], KV.at[slot, :, rows]
            return remote(src, dst, s_k.at[slot, part, 0], r_k.at[slot, part, 0], k_dev[slot])
        src, dst = KV.at[2 - what, what, rows], KV.at[3, what, rows]
        return remote(src, dst, s_k.at[3, part, what], r_k.at[3, part, what], k_dev[2 - what])

    def add_block(qs, q_lo, ks, k_lo, mask, queries=HALF, keys=HALF):
        q_rows, k_rows = pl.ds(q_lo, queries), pl.ds(k_lo, keys)
        dq, dk, dv = block(
            QD[qs, 0, q_rows, :],
            QD[qs, 1, q_rows, :],
            ST[qs, :, q_rows],
            KV[ks, 0, k_rows, :],
            KV[ks, 1, k_rows, :],
            mask,
            (0, 1),
        )
        for e, part in dq:
            DQ[qs, e * HEAD : (e + 1) * HEAD, q_rows] += part
        DKV[ks, 0, k_rows, :] += dk
        DKV[ks, 1, k_rows, :] += dv

    def visible_lower(qs, ks):
        q_outer = ((x_hi + qs // 2) % 2) * 2 + (core + qs % 2) % 2
        k_inner = (inner + (ks + 1) // 2 + 2 * ((ks % 2) * (1 - ks // 2))) % 4
        return order[2 * (k_inner * 4 + outer)] < order[2 * (inner * 4 + q_outer)]

    def add_pair(qs, ks, heads=(0, 1)):
        sel = visible_lower(qs, ks)

        def pick(lo, hi):
            return jnp.where(sel, lo, hi)

        q, do, stats = QD[qs, 0], QD[qs, 1], ST[qs]
        k, v = KV[ks, 0], KV[ks, 1]
        dq, dk, dv = block(q[HALF:], do[HALF:], stats[:, HALF:], k[:HALF], v[:HALF], False, heads)
        dq2, dk2, dv2 = block(
            pick(q[:HALF], q[HALF:]),
            pick(do[:HALF], do[HALF:]),
            pick(stats[:, :HALF], stats[:, HALF:]),
            pick(k[:HALF], k[HALF:]),
            pick(v[:HALF], v[HALF:]),
            False,
            heads,
        )
        for (e, upper), (_, part) in zip(dq, dq2):
            zero = jnp.zeros_like(part)
            rows = slice(e * HEAD, (e + 1) * HEAD)
            DQ[qs, rows, 0:HALF] += jnp.where(sel, part, zero)
            DQ[qs, rows, HALF:ROWS] += upper + jnp.where(sel, zero, part)
        for j, (lower, part) in enumerate(((dk, dk2), (dv, dv2))):
            zero = jnp.zeros_like(part)
            DKV[ks, j, 0:HALF, :] += lower + jnp.where(sel, part, zero)
            DKV[ks, j, HALF:ROWS, :] += jnp.where(sel, zero, part)

    def own_diagonal(which):
        at = pl.multiple_of(which * HALF, HALF)
        add_block(0, at, 0, at, True, HALF, TILE)
        at = pl.multiple_of(which * HALF + TILE, TILE)
        add_block(0, at, 0, at, True, TILE, TILE)

    def wait_half(part, kinds):
        base = 4 * ((1 - x_lo) if part == HI else x_lo)
        for j in range(4):

            def arrived(r=base + j):
                for kind in kinds:
                    exchange(kind, r).wait_recv()

            if j == 0:
                pl.when(base > 0)(arrived)
            else:
                arrived()

    def near_keys(part):
        for slot in (1, 2):
            send_k(slot, part, 0).wait_recv()
            send_k(3, part, 2 - slot).start()

    for r in turn:
        exchange(1, r).wait_send()
    for r in (1, 3, 2, 4, 5, 7, 6):
        for i in (0, 1):
            if r < 4:
                fetch(r, i).wait()
        exchange(0, r).start()
    lax.fori_loop(0, 8, clear, 0)
    for i in range(4):
        fetch(0, i).wait()
    for part, group in ((x_lo, (1, 2, 3)), (1 - x_lo, (4, 5, 6, 7))):
        for r in group:
            exchange(1, r).wait_recv()
        for slot in (1, 2):
            send_k(slot, part, 0).start()
    near_keys(x_lo)
    own_stat.wait()
    for part, group in ((x_lo, (1, 2, 3)), (1 - x_lo, (4, 5, 6, 7))):
        for r in group:
            for kind in (2, 0):
                exchange(kind, r).wait_recv()
        for what in (1, 0):
            send_q(1, part, what).start()
        if group[0] == 1:
            own_diagonal(x_lo)
    to_stage().wait_recv()
    for b in (1, 3, 2):
        from_stage(b).start()
        to_far(0, b).start()
    to_far(0, 0).start()

    def arrived_queries(slot, part):
        for what in (1, 0):
            send_q(slot, part, what).wait_recv()

    def far_to_core(part):
        crossed = (1 - x_lo) if part == HI else x_lo

        @pl.when(crossed == 1)
        def _():
            to_far_in(0, 4).wait_recv()
            for b in (1, 2, 3):
                from_stage(b).wait_recv()

        @pl.when(crossed == 0)
        def _():
            for r in range(4):
                to_far_in(0, r).wait_recv()

        for j in range(4):
            to_far_in(1, 4 * crossed + j).wait_recv()
        for what in (1, 0):
            send_q(3, part, what).start()

    def to_far_in(kind, r):
        dst = (ST if kind else QD).at[2, :, mine]
        return remote(dst, dst, s_far.at[kind, r], r_far.at[kind, r], (head, inner, far_outer))

    def return_core(slot, e):
        feats = pl.ds(e * HEAD, HEAD)
        src, dst = DQ.at[slot, feats], core_recv.at[slot // 2, feats]
        return remote(src, dst, s_dq.at[slot, e], r_dq.at[slot, e], core_dev)

    def return_dkv(slot, j):
        src, dst = dkv_send.at[slot - 1, j], dkv_recv.at[slot - 1, j]
        return remote(src, dst, s_dk.at[slot, j], r_dk.at[slot, j], back_dev[slot])

    own_diagonal(1 - x_lo)
    add_block(0, HALF, 0, 0, False)
    near_keys(1 - x_lo)
    for part in (HI, LO):
        arrived_queries(1, part)
    add_pair(1, 0)

    def near_queries(n, _):
        qs, ks = n % 2, 1 + n // 2

        for at, part in ((4, HI), (5, LO)):

            @pl.when(n == at)
            def _():
                far_to_core(part)

        @pl.when(n == 4)
        def _():
            for part in (LO, HI):
                for what in range(2):
                    send_k(3, part, what).wait_recv()

        add_pair(qs, ks)
        return 0

    lax.fori_loop(0, 6, near_queries, 0)

    for e in range(2):
        return_core(1, e).start()
    back = (4, 1, 5, 3, 7, 2, 6, 0)

    def transpose_dq(far, e, r):
        rows, feats = wide(peer(r), PART), slice(e * HEAD, (e + 1) * HEAD)
        total = DQ[2 * far, feats, rows] + core_recv[far, feats, rows]
        dq_fin[far, e, rows, :] = (total * SCALE).T.astype(BF16)

    def give_dq(far, e, r):
        p = peer(r)
        src, dst = dq_fin.at[far, e, wide(p, PART)], dq_part.at[far, head, e]
        if not far and r == 0:
            return pltpu.make_async_copy(src, dst, s_dqo.at[0, e, 0])
        device = (p, inner, far_outer if far else outer)
        return remote(src, dst, s_dqo.at[far, e, r], r_dqo.at[far, e, r], device)

    def send_rows(far, e):
        return_core(3 if far else 1, e).wait_recv()
        for r in back:
            transpose_dq(far, e, r)
            give_dq(far, e, r).start()

    def far_queries(m, _):
        i = m // 2
        qs, ks = 2 + m % 2, i + 3 * ((3 - i) // 3)

        @pl.when(m == 1)
        def _():
            for part in (HI, LO):
                arrived_queries(3, part)

        add_pair(qs, ks)
        @pl.when(m == 1)
        def _():
            for e in range(2):
                send_rows(0, e)

        for at, slot in ((1, 3), (3, 1), (5, 2)):

            @pl.when(m == at)
            def _():
                for j in range(2):

                    def step(i, _):
                        rows = pl.ds(pl.multiple_of(i * 128, 128), 128)
                        dkv_send[slot - 1, j, rows, :] = DKV[slot, j, rows, :].astype(BF16)
                        return 0

                    lax.fori_loop(0, 8, step, 0)
                    return_dkv(slot, j).start()

        return 0

    lax.fori_loop(0, 6, far_queries, 0)

    for e in range(2):
        add_pair(3, 0, (e,))
        return_core(3, e).start()
        if e == 1:
            send_rows(1, 0)
        add_pair(2, 0, (e,))
    send_rows(1, 1)

    def give(kind, r):
        p = peer(r)
        src, dst = dkv_fin.at[kind, wide(p, PART)], (dk_out, dv_out)[kind].at[0, :, wide(head, HEAD)]
        if r == 0:
            return pltpu.make_async_copy(src, dst, s_out.at[kind, 0])
        return remote(src, dst, s_out.at[kind, r], r_out.at[kind, r], (p, inner, outer))

    for j, scale in ((0, SCALE), (1, 1.0)):
        for slot in (3, 1, 2):
            return_dkv(slot, j).wait_recv()
        for r in back:
            rows = wide(peer(r), PART)
            total = DKV[0, j, rows, :]
            for slot in range(3):
                total = total + dkv_recv[slot, j, rows, :].astype(F32)
            dkv_fin[j, rows, :] = (total * scale).astype(BF16)
            give(j, r).start()

    for e in range(2):
        for far in range(2):
            for r in range(8):
                give_dq(far, e, r).wait()
        for g in range(HEADS):
            total = dq_part[0, g, e].astype(F32) + dq_part[1, g, e].astype(F32)
            dq_out[0, :, g * 256 + e * HEAD : g * 256 + (e + 1) * HEAD] = total.astype(BF16)

    for r in range(1, 8):
        for i in (0, 2):
            exchange(i, r).wait_send()
    for r in range(8):
        to_far(1, r).wait_send()
    for r in range(5):
        to_far(0, r).wait_send()
    to_stage().wait_send()
    for b in (1, 2, 3):
        from_stage(b).wait_send()
    for slot in (1, 2, 3):
        for part in range(2):
            for what in range(2):
                if slot != 2:
                    send_q(slot, part, what).wait_send()
            for what in range(2 if slot == 3 else 1):
                send_k(slot, part, what).wait_send()
        for j in range(2):
            return_dkv(slot, j).wait_send()
    for slot in (1, 3):
        for e in range(2):
            return_core(slot, e).wait_send()
    for kind in range(2):
        for r in range(8):
            give(kind, r).wait()


def copy_kernel(dq, dk, dv, dq_out, dk_out, dv_out, dq_vm, dk_vm, dv_vm, sem):
    steps = []
    for i, (src, via, dst) in enumerate(((dq, dq_vm, dq_out), (dk, dk_vm, dk_out), (dv, dv_vm, dv_out))):
        for j in range(2):
            rows = pl.ds(j * PART // 2, PART // 2)
            n = 2 * i + j
            arrive = pltpu.make_async_copy(src.at[:, rows], via.at[:, rows], sem.at[0, n])
            leave = pltpu.make_async_copy(via.at[:, rows], dst.at[:, rows], sem.at[1, n])
            steps.append((arrive, leave))
    for arrive, _ in steps:
        arrive.start()
    for arrive, leave in steps:
        arrive.wait()
        leave.start()
    for _, leave in steps:
        leave.wait()


def per_device(queries, key_input, value_input, outputs, output_gradient, log_sum_exp, block_order):
    any_space = pl.BlockSpec(memory_space=pl.ANY)
    dma = pltpu.SemaphoreType.DMA
    grads = pl.pallas_call(
        kernel,
        out_shape=(
            jax.ShapeDtypeStruct((1, PART, 2048), BF16),
            jax.ShapeDtypeStruct((1, PART, 1024), BF16),
            jax.ShapeDtypeStruct((1, PART, 1024), BF16),
        ),
        in_specs=[pl.BlockSpec(memory_space=pltpu.SMEM)]
        + [any_space] * 5
        + [pl.BlockSpec(memory_space=pltpu.VMEM)],
        out_specs=(pl.BlockSpec(memory_space=pltpu.VMEM), any_space, any_space),
        scratch_shapes=[
            pltpu.VMEM((PART, 2048), BF16),
            pltpu.VMEM((PART, 2048), BF16),
            pltpu.VMEM((HEADS, 2, PART, 256), BF16),
            pltpu.VMEM((HEADS, 2, PART, HEAD), BF16),
            pltpu.VMEM((HEADS, 8, PART), F32),
            pltpu.VMEM((3, 2, PART, 256), BF16),
            pltpu.VMEM((4, 2, ROWS, 256), BF16),
            pltpu.VMEM((4, 2, ROWS, HEAD), BF16),
            pltpu.VMEM((4, 8, ROWS), F32),
            pltpu.VMEM((4, 256, ROWS), F32),
            pltpu.VMEM((4, 2, ROWS, HEAD), F32),
            pltpu.VMEM((3, 2, ROWS, HEAD), BF16),
            pltpu.VMEM((3, 2, ROWS, HEAD), BF16),
            pltpu.VMEM((2, 256, ROWS), F32),
            pltpu.VMEM((2, 2, ROWS, HEAD), BF16),
            pltpu.VMEM((2, HEADS, 2, PART, HEAD), BF16),
            pltpu.VMEM((2, ROWS, HEAD), BF16),
            dma((5, 8)),
            dma((3, 8)),
            dma((3, 8)),
            dma((4, 2, 2)),
            dma((4, 2, 2)),
            dma((4, 2, 2)),
            dma((4, 2, 2)),
            dma((4, 2)),
            dma((4, 2)),
            dma((4, 2)),
            dma((4, 2)),
            dma((2, 8)),
            dma((2, 8)),
            dma((4,)),
            dma((4,)),
            dma((2, 2, 8)),
            dma((2, 2, 8)),
            dma((2, 8)),
            dma((2, 8)),
        ],
        compiler_params=pltpu.CompilerParams(
            collective_id=0, has_side_effects=True, vmem_limit_bytes=56 * 1024 * 1024
        ),
        name="attention_backward",
    )(block_order, queries, key_input, value_input, outputs, output_gradient, jnp.transpose(log_sum_exp, (0, 2, 1)))
    return pl.pallas_call(
        copy_kernel,
        out_shape=tuple(jax.ShapeDtypeStruct(g.shape, g.dtype) for g in grads),
        in_specs=[any_space] * 3,
        out_specs=(any_space,) * 3,
        scratch_shapes=[pltpu.VMEM(g.shape, g.dtype) for g in grads] + [dma((2, 6))],
        name="copy_out",
    )(*grads)


def solution(mesh):
    split = P(("inner", "outer"), "head", None)
    return jax.shard_map(
        per_device, mesh=mesh, in_specs=(split,) * 6 + (P(),), out_specs=(split,) * 3, check_vma=False
    )
```
